32 devices in a mesh: group: 2 (over y), tp: 8 (over z, x), dp: 2 (over core).
Axes of the slice: x: 2, y: 2, z: 4, core: 2. Of those that a mesh axis runs over, the one named last changes fastest.
Arguments:
- hidden: bfloat16 [4, 384, 2, 8192], P(('group', 'dp'), None, None, 'tp'), parts along dimension 0, may hold values from -8 to 8
- norm_gain: bfloat16 [8192], replicated, may hold values from 0.5 to 1.5
- w_qkv: bfloat16 [8192, 64, 160], P(None, 'tp'), may hold values from -0.0625 to 0.0625
- adapter_store: bfloat16 [96, 8192, 128], P(('group', 'tp', 'dp')), parts along dimension 0, may hold values from -0.75 to 0.75
- adapter_home: int32 [96], P('group'), parts along dimension 0, may hold values from 0 to 47, as said below
- slot_adapter: int32 [4, 8], P('group'), parts along dimension 0, may hold values from 0 to 47, as said below
- request_slot: int32 [4, 384], P(('group', 'dp')), parts along dimension 0, may hold values from 0 to 7, as said below
- cache_kv: bfloat16 [4, 384, 128, 2048], P(('group', 'dp'), 'tp'), parts along dimension 0, may hold values from -240 to 240
- cache_len: int32 [4, 384], P(('group', 'dp'), 'tp'), parts along dimension 0, may hold values from 1 to 128
Outputs:
- attn_out: bfloat16 [4, 384, 2, 8192], P(('group', 'dp'), 'tp'), parts along dimension 0
- new_kv: bfloat16 [4, 384, 2, 2048], P(('group', 'dp'), 'tp'), parts along dimension 0
The draws below stay inside these ranges and needn't reach their ends.
There are 2 independent parts, one for each index of `group`. The reference program is written for one: setup_inputs(seed, part) draws one part's arguments, and reference() takes and returns one part's arrays. A program takes and returns all parts, laid end to end along the dimension named above; an argument that names none is the same for every part. Nothing has to cross between parts.
Inputs may be any that keep to these rules, and one draw needn't show every extreme that they name: `adapter_home`: a permutation of the storage rows. Within one block, the numbers adapter_home[slot_adapter[n, s]] // 6 over its 8 slots are all different. `request_slot`: every slot of a block is used by some request of that block.
All inputs are finite; a program needn't handle non-finite values.
Results may differ from the reference program's by a relative error of at most 0.0031.
The reference program's roundings to bfloat16 on the way count: a program that leaves them out, or rounds other values in their place, can miss the bound.
Values may be sent and summed in bfloat16 or wider, within the bound.
A program may use at most 256 MiB of HBM per device.

```python
import jax
import jax.numpy as jnp
from jax import lax

D = 8192
HEADS = 64
KV_HEADS = 8
HEAD_WIDTH = 128
RANK = 64
REQ_DEV = 384
CACHE = 128
ADAPT_DEV = 3
KEY_VALUE_SHARE = 32
GROUP = 8
SLOTS = 8
NADAPT = 48
N_DP = 2


def skewed_index(key, shape, limit):
    first_key, second_key = jax.random.split(key)
    first_draw = jax.random.randint(first_key, shape, 0, limit)
    second_draw = jax.random.randint(second_key, shape, 0, limit)
    return first_draw * second_draw // limit


def permute_rows(key, count, length):

    def permute_one(subkey):
        return jax.random.permutation(subkey, length)
    return jax.vmap(permute_one)(jax.random.split(key, count))


def layout(key):
    home_key, column_key, within_key = jax.random.split(key, 3)
    home_rows = jax.random.permutation(home_key, NADAPT).astype(jnp.int32)
    inverse = jnp.argsort(home_rows).astype(jnp.int32)
    per_column = N_DP * ADAPT_DEV
    columns = permute_rows(column_key, N_DP, SLOTS).astype(jnp.int32)
    within = skewed_index(within_key, (N_DP, SLOTS), per_column).astype(jnp.int32)
    storage_rows = columns * per_column + within
    return (home_rows, inverse[storage_rows])


def draw_adapter_home(key, part):
    return layout(key)[0]


def draw_slot_adapter(key, part):
    return layout(key)[1].astype(jnp.int32)


def draw_request_slot(key, part):
    key = jax.random.fold_in(key, 3)
    skew_key, rank_key = jax.random.split(key)
    skewed = skewed_index(skew_key, (N_DP, REQ_DEV), SLOTS)
    ranking = permute_rows(rank_key, N_DP, REQ_DEV)
    return jnp.where(ranking < SLOTS, ranking, skewed).astype(jnp.int32)


def draw_cache_len(key, part):
    key = jax.random.fold_in(key, 5)
    first_key, second_key = jax.random.split(key)
    first_draw = jax.random.randint(first_key, (N_DP, REQ_DEV), 1, CACHE + 1)
    second_draw = jax.random.randint(second_key, (N_DP, REQ_DEV), 1, CACHE + 1)
    shorter = jnp.minimum(first_draw, second_draw)
    return shorter.at[:, 0].set(CACHE).at[:, 1].set(1).astype(jnp.int32)


def draw_cache_kv(key, part):
    key = jax.random.fold_in(key, 11)
    sample_key = jax.random.fold_in(key, 0)
    samples = jax.random.truncated_normal(sample_key, -6.0, 6.0, (N_DP, REQ_DEV, CACHE, 2 * KV_HEADS * HEAD_WIDTH), jnp.float32)
    return samples.astype(jnp.bfloat16)


def spiked(drawn, rng, source, target, blocks, factor):
    owner, partner = [(jnp.arange(drawn.shape[axis_at]) // (drawn.shape[axis_at] // blocks)).reshape([-1 if axis == axis_at else 1 for axis in range(drawn.ndim)]) for axis_at in (source, target)]
    chosen = jax.random.permutation(rng, blocks)[partner]
    strong = (owner == chosen) | (owner == (partner + blocks // 2) % blocks)
    return jnp.where(strong, factor * drawn, drawn)


def steps_of(own_key, extent, pieces, least, largest):
    level, own = 1.0, jax.random.fold_in(own_key, 6)
    for position, blocks in pieces:
        steps = jnp.exp(jax.random.uniform(jax.random.fold_in(own, position), (blocks,), jnp.float32, least / len(pieces), largest / len(pieces)))
        level = level * jnp.repeat(steps, extent[position] // blocks).reshape([-1 if axis == position else 1 for axis in range(len(extent))])
    return level


def bell_draw(stream_key, shape, deviation, bound, pieces=(), kind=jnp.bfloat16):
    drawn = deviation * jax.random.normal(stream_key, shape, jnp.float32)
    if pieces:
        drawn = drawn * steps_of(stream_key, shape, pieces, -0.22, 0.18)
    return jnp.clip(drawn, -bound, bound).astype(kind)


def bell_draw_with(key, extent, scale, reach, pieces, heavy, kind=jnp.bfloat16):
    result = scale * jax.random.normal(key, extent, jnp.float32)
    if pieces:
        result = result * steps_of(key, extent, pieces, -0.22, 0.18)
    return jnp.clip(spiked(result, jax.random.fold_in(key, 3), *heavy), -reach, reach).astype(kind)


def setup_inputs(seed: int = 0, part: int = 0) -> dict:
    arg_keys = jax.random.split(jax.random.key(seed), 10)
    part_splits = jax.random.split(jax.random.fold_in(arg_keys[9], part), 10)
    return {
        "hidden": bell_draw_with(part_splits[0], (N_DP, REQ_DEV, 2, D), 1.0, 8.0, ((0, 2), (3, 8)), (3, 1, 8, 2.0)),
        "norm_gain": jnp.clip(1.0 + 0.1 * jax.random.normal(arg_keys[1], (D,), jnp.float32), 0.5, 1.5).astype(jnp.bfloat16),
        "w_qkv": bell_draw(arg_keys[2], (D, HEADS, HEAD_WIDTH + KEY_VALUE_SHARE), D ** -0.5, 0.0625, ((1, 8),)),
        "adapter_store": bell_draw(part_splits[3], (NADAPT, D, 2 * RANK), RANK ** -0.5, 0.75, ((0, 16),)),
        "adapter_home": draw_adapter_home(jax.random.fold_in(jax.random.fold_in(arg_keys[9], part), 71), part),
        "slot_adapter": draw_slot_adapter(jax.random.fold_in(jax.random.fold_in(arg_keys[9], part), 71), part),
        "request_slot": draw_request_slot(jax.random.fold_in(jax.random.fold_in(arg_keys[9], part), 71), part),
        "cache_kv": draw_cache_kv(jax.random.fold_in(jax.random.fold_in(arg_keys[9], part), 71), part),
        "cache_len": draw_cache_len(jax.random.fold_in(jax.random.fold_in(arg_keys[9], part), 71), part),
    }


adapter_scale = 0.0625
rope_base = 500000.0
norm_eps = 1e-05
masked_out = -1e+30

def rotate(vectors, positions):
    halfway = vectors.shape[-1] // 2
    counter = jnp.arange(halfway, dtype=jnp.float32)
    inverse_freq = rope_base ** (-2.0 * counter / vectors.shape[-1])
    angles = positions[..., None] * inverse_freq
    cosine = jnp.cos(angles)
    sine_part = jnp.sin(angles)
    leading = vectors[..., :halfway]
    trailing = vectors[..., halfway:]
    return jnp.concatenate([leading * cosine - trailing * sine_part, trailing * cosine + leading * sine_part], axis=-1)

def attend(query_rot, key_rot, value_new, cache_block, length_block):
    batch_count = query_rot.shape[0]
    grouped = query_rot.astype(jnp.float32).reshape(batch_count, 2, KV_HEADS, GROUP, HEAD_WIDTH)
    cached = cache_block.astype(jnp.float32)
    cache_keys = cached[:, :, :KV_HEADS * HEAD_WIDTH].reshape(batch_count, CACHE, KV_HEADS, HEAD_WIDTH)
    cache_values = cached[:, :, KV_HEADS * HEAD_WIDTH:].reshape(batch_count, CACHE, KV_HEADS, HEAD_WIDTH)
    factor = HEAD_WIDTH ** (-0.5)
    old_scores = jnp.einsum('rpgjc,rlgc->rpgjl', grouped, cache_keys) * factor
    new_scores = jnp.einsum('rpgjc,rngc->rpgjn', grouped, key_rot.astype(jnp.float32)) * factor
    old_valid = jnp.arange(CACHE, dtype=jnp.int32)[None, :] < length_block[:, None]
    new_valid = jnp.arange(2, dtype=jnp.int32)[None, :] <= jnp.arange(2, dtype=jnp.int32)[:, None]
    old_scores = jnp.where(old_valid[:, None, None, None, :], old_scores, masked_out)
    new_scores = jnp.where(new_valid[None, :, None, None, :], new_scores, masked_out)
    highest = jnp.maximum(lax.optimization_barrier(jnp.max(old_scores, axis=-1)), lax.optimization_barrier(jnp.max(new_scores, axis=-1)))[..., None]
    old_exp = jnp.exp(old_scores - highest)
    new_exp = jnp.exp(new_scores - highest)
    denominator = lax.optimization_barrier(jnp.sum(old_exp, axis=-1, keepdims=True)) + lax.optimization_barrier(jnp.sum(new_exp, axis=-1, keepdims=True))
    old_weights = (old_exp / denominator).astype(jnp.bfloat16)
    new_weights = (new_exp / denominator).astype(jnp.bfloat16)
    mixture = jnp.einsum('rpgjl,rlgc->rpgjc', old_weights.astype(jnp.float32), cache_values)
    mixture = mixture + jnp.einsum('rpgjn,rngc->rpgjc', new_weights.astype(jnp.float32), value_new.astype(jnp.float32))
    return mixture.astype(jnp.bfloat16).reshape(batch_count, 2, HEADS * HEAD_WIDTH)

def attend_block(grouped_operands):
    return attend(*grouped_operands)

def reference(hidden, norm_gain, w_qkv, adapter_store, adapter_home, slot_adapter, request_slot, cache_kv, cache_len):
    widened = hidden.astype(jnp.float32)
    mean_square = lax.optimization_barrier(jnp.mean(widened * widened, axis=-1, keepdims=True))
    normed = (widened * lax.rsqrt(mean_square + norm_eps) * norm_gain.astype(jnp.float32)).astype(jnp.bfloat16)
    row_block = normed.reshape(N_DP, REQ_DEV * 2, D)
    columns = HEADS * (HEAD_WIDTH + KEY_VALUE_SHARE)
    projected_rows = jnp.dot(row_block.reshape(N_DP * REQ_DEV * 2, D), w_qkv.reshape(D, columns), preferred_element_type=jnp.float32)
    projected_rows = projected_rows.reshape(N_DP, REQ_DEV, 2, HEADS, HEAD_WIDTH + KEY_VALUE_SHARE)
    stored_rows = adapter_home[slot_adapter]

    def adapter_delta(operands):
        block_rows, block_stored, block_slot = operands
        adapters = adapter_store[block_stored]
        down_matrix = jnp.transpose(adapters[:, :, :RANK], (1, 0, 2)).reshape(D, SLOTS * RANK)
        partial_rank = jnp.dot(block_rows, down_matrix, preferred_element_type=jnp.float32).reshape(REQ_DEV * 2, SLOTS, RANK)
        row_slot = jnp.repeat(block_slot, 2)
        chosen = row_slot[:, None] == jnp.arange(SLOTS, dtype=jnp.int32)[None, :]
        lowrank = lax.optimization_barrier(jnp.sum(jnp.where(chosen[:, :, None], partial_rank, 0.0), axis=1)).astype(jnp.bfloat16)
        spread = jnp.where(chosen[:, :, None], lowrank[:, None, :], jnp.zeros((), jnp.bfloat16)).reshape(REQ_DEV * 2, SLOTS * RANK)
        up_matrix = jnp.transpose(adapters[:, :, RANK:], (0, 2, 1)).reshape(SLOTS * RANK, D)
        return jnp.dot(spread, up_matrix, preferred_element_type=jnp.float32)
    delta_query = lax.map(adapter_delta, (row_block, stored_rows, request_slot))
    delta_query = delta_query.reshape(N_DP, REQ_DEV, 2, HEADS, HEAD_WIDTH)
    delta_padded_rows = jnp.pad(delta_query, ((0, 0), (0, 0), (0, 0), (0, 0), (0, KEY_VALUE_SHARE)))
    packed_columns = (projected_rows + adapter_scale * delta_padded_rows).astype(jnp.bfloat16)
    query_part = packed_columns[..., :HEAD_WIDTH]
    shared = packed_columns[..., HEAD_WIDTH:].reshape(N_DP, REQ_DEV, 2, HEADS * KEY_VALUE_SHARE)
    key_new = shared[..., :KV_HEADS * HEAD_WIDTH].reshape(N_DP, REQ_DEV, 2, KV_HEADS, HEAD_WIDTH)
    value_new = shared[..., KV_HEADS * HEAD_WIDTH:].reshape(N_DP, REQ_DEV, 2, KV_HEADS, HEAD_WIDTH)
    positions = (cache_len[:, :, None] + jnp.arange(2, dtype=jnp.int32)[None, None, :]).astype(jnp.float32)
    query_rot = rotate(query_part.astype(jnp.float32), positions[..., None]).astype(jnp.bfloat16)
    key_rot = rotate(key_new.astype(jnp.float32), positions[..., None]).astype(jnp.bfloat16)
    new_kv = jnp.concatenate([key_rot.reshape(N_DP, REQ_DEV, 2, KV_HEADS * HEAD_WIDTH), value_new.reshape(N_DP, REQ_DEV, 2, KV_HEADS * HEAD_WIDTH)], axis=-1)
    total_requests = N_DP * REQ_DEV
    block_size = 64 if total_requests % 64 == 0 else total_requests
    block_count = total_requests // block_size

    def regroup(source):
        return source.reshape((block_count, block_size) + source.shape[2:])
    operands = (regroup(query_rot), regroup(key_rot), regroup(value_new), regroup(cache_kv), regroup(cache_len))
    attended = lax.map(attend_block, operands)
    attn_out = attended.reshape(N_DP, REQ_DEV, 2, HEADS * HEAD_WIDTH)
    return (attn_out, new_kv)
```

```python
import functools

import jax
import jax.numpy as jnp
from jax import lax
from jax.experimental import pallas as pl
from jax.experimental.pallas import tpu as pltpu
from jax.sharding import PartitionSpec as P

D = 8192
HEADS = 64
KV_HEADS = 8
HEAD_WIDTH = 128
RANK = 64
CACHE = 128
ADAPT_DEV = 3
KEY_VALUE_SHARE = 32
GROUP = 8


adapter_scale = 0.0625
rope_base = 500000.0
norm_eps = 1e-05
masked_out = -1e30


def rotate(vectors, positions):
    halfway = vectors.shape[-1] // 2
    counter = jnp.arange(halfway, dtype=jnp.float32)
    inverse_freq = rope_base ** (-2.0 * counter / vectors.shape[-1])
    angles = positions[..., None] * inverse_freq
    cosine = jnp.cos(angles)
    sine_part = jnp.sin(angles)
    leading = vectors[..., :halfway]
    trailing = vectors[..., halfway:]
    return jnp.concatenate(
        [leading * cosine - trailing * sine_part, trailing * cosine + leading * sine_part], axis=-1
    )


def attend(query_rot, key_rot, value_new, cache_block, length_block):
    batch_count = query_rot.shape[0]
    grouped = query_rot.reshape(batch_count, 2, KV_HEADS, GROUP, HEAD_WIDTH)
    cache_keys = cache_block[:, :, : KV_HEADS * HEAD_WIDTH].reshape(
        batch_count, CACHE, KV_HEADS, HEAD_WIDTH
    )
    cache_values = cache_block[:, :, KV_HEADS * HEAD_WIDTH :].reshape(
        batch_count, CACHE, KV_HEADS, HEAD_WIDTH
    )
    factor = HEAD_WIDTH ** (-0.5)
    old_scores = (
        jnp.einsum("rpgjc,rlgc->rpgjl", grouped, cache_keys, preferred_element_type=jnp.float32)
        * factor
    )
    new_scores = (
        jnp.einsum("rpgjc,rngc->rpgjn", grouped, key_rot, preferred_element_type=jnp.float32)
        * factor
    )
    old_valid = jnp.arange(CACHE, dtype=jnp.int32)[None, :] < length_block[:, None]
    new_valid = jnp.arange(2, dtype=jnp.int32)[None, :] <= jnp.arange(2, dtype=jnp.int32)[:, None]
    old_scores = jnp.where(old_valid[:, None, None, None, :], old_scores, masked_out)
    new_scores = jnp.where(new_valid[None, :, None, None, :], new_scores, masked_out)
    highest = jnp.maximum(jnp.max(old_scores, axis=-1), jnp.max(new_scores, axis=-1))[..., None]
    old_exp = jnp.exp(old_scores - highest)
    new_exp = jnp.exp(new_scores - highest)
    denominator = jnp.sum(old_exp, axis=-1, keepdims=True) + jnp.sum(
        new_exp, axis=-1, keepdims=True
    )
    old_weights = (old_exp / denominator).astype(jnp.bfloat16)
    new_weights = (new_exp / denominator).astype(jnp.bfloat16)
    mixture = jnp.einsum(
        "rpgjl,rlgc->rpgjc", old_weights, cache_values, preferred_element_type=jnp.float32
    )
    mixture = mixture + jnp.einsum(
        "rpgjn,rngc->rpgjc", new_weights, value_new, preferred_element_type=jnp.float32
    )
    return mixture.astype(jnp.bfloat16).reshape(batch_count, 2, HEADS * HEAD_WIDTH)


def slot_delta(slot_slices, local_normed, chosen, count_of_rows, slot_count, local_width):
    down_matrix = jnp.transpose(slot_slices[:, :, :RANK], (1, 0, 2)).reshape(
        local_width, slot_count * RANK
    )
    partial_rank = jnp.dot(local_normed, down_matrix, preferred_element_type=jnp.float32).reshape(
        count_of_rows, slot_count, RANK
    )
    partial_rank = jnp.sum(jnp.where(chosen[:, :, None], partial_rank, 0.0), axis=1)
    lowrank = lax.psum(partial_rank, "tp").astype(jnp.bfloat16)
    spread = jnp.where(
        chosen[:, :, None], lowrank[:, None, :], jnp.zeros((), jnp.bfloat16)
    ).reshape(count_of_rows, slot_count * RANK)
    up_matrix = jnp.transpose(slot_slices[:, :, RANK:], (0, 2, 1)).reshape(
        slot_count * RANK, local_width
    )
    return jnp.dot(spread, up_matrix, preferred_element_type=jnp.float32)


def plain_body(
    hidden,
    norm_gain,
    w_qkv,
    adapter_store,
    adapter_home,
    slot_adapter,
    request_slot,
    cache_kv,
    cache_len,
):
    tp_count = lax.axis_size("tp")
    dp_count = lax.axis_size("dp")
    tp_index = lax.axis_index("tp")
    dp_index = lax.axis_index("dp")
    requests = hidden.shape[1]
    local_width = hidden.shape[3]
    device_heads = w_qkv.shape[1]
    slot_count = slot_adapter.shape[1]
    count_of_rows = requests * 2
    flat_rows = hidden[0].reshape(count_of_rows, local_width)
    gain_wide = norm_gain.astype(jnp.float32)
    weights = w_qkv.reshape(D, device_heads * (HEAD_WIDTH + KEY_VALUE_SHARE))
    column_start = tp_index * local_width
    stored_rows = adapter_home[slot_adapter]
    block_rows = lax.dynamic_index_in_dim(stored_rows, dp_index, 0, keepdims=False)
    device_index = tp_index * dp_count + dp_index
    offsets = stored_rows - device_index * ADAPT_DEV
    local_slots = jnp.arange(ADAPT_DEV, dtype=jnp.int32)
    selector = jnp.any(offsets[:, :, None] == local_slots[None, None, :], axis=1).astype(
        jnp.bfloat16
    )
    row_slot = jnp.repeat(request_slot[0], 2)
    chosen = row_slot[:, None] == jnp.arange(slot_count, dtype=jnp.int32)[None, :]
    gathered = lax.all_gather(flat_rows, "tp", axis=1, tiled=True)
    widened = gathered.astype(jnp.float32)
    mean_square = jnp.mean(widened * widened, axis=1, keepdims=True)
    normed = (widened * lax.rsqrt(mean_square + norm_eps) * gain_wide).astype(jnp.bfloat16)
    local_normed = lax.dynamic_slice_in_dim(normed, column_start, local_width, 1)
    projected_whole = jnp.dot(normed, weights, preferred_element_type=jnp.float32)
    pieces = adapter_store.reshape(ADAPT_DEV, tp_count, local_width, 2 * RANK)
    outgoing = jnp.einsum(
        "bm,mtlk->tblk", selector, pieces, preferred_element_type=jnp.float32
    ).astype(jnp.bfloat16)
    outgoing = outgoing.reshape(tp_count * dp_count, local_width, 2 * RANK)
    incoming = lax.all_to_all(outgoing, ("tp", "dp"), split_axis=0, concat_axis=0, tiled=True)
    slot_slices = jnp.take(incoming, block_rows // ADAPT_DEV, axis=0)
    delta_query = slot_delta(
        slot_slices, local_normed, chosen, count_of_rows, slot_count, local_width
    )
    delta_padded_rows = jnp.pad(
        delta_query.reshape(count_of_rows, device_heads, HEAD_WIDTH),
        ((0, 0), (0, 0), (0, KEY_VALUE_SHARE)),
    )
    packed_columns = (
        projected_whole.reshape(count_of_rows, device_heads, HEAD_WIDTH + KEY_VALUE_SHARE)
        + adapter_scale * delta_padded_rows
    ).astype(jnp.bfloat16)
    packed_columns = packed_columns.reshape(requests, 2, device_heads, HEAD_WIDTH + KEY_VALUE_SHARE)
    arrived_heads = lax.all_to_all(packed_columns, "tp", split_axis=0, concat_axis=2, tiled=True)
    local_requests = arrived_heads.shape[0]
    query_part = arrived_heads[..., :HEAD_WIDTH]
    shared = arrived_heads[..., HEAD_WIDTH:].reshape(local_requests, 2, HEADS * KEY_VALUE_SHARE)
    key_new = shared[..., : KV_HEADS * HEAD_WIDTH].reshape(local_requests, 2, KV_HEADS, HEAD_WIDTH)
    value_new = shared[..., KV_HEADS * HEAD_WIDTH :].reshape(
        local_requests, 2, KV_HEADS, HEAD_WIDTH
    )
    lengths = cache_len[0]
    positions = (lengths[:, None] + jnp.arange(2, dtype=jnp.int32)[None, :]).astype(jnp.float32)
    query_rot = rotate(query_part.astype(jnp.float32), positions[..., None]).astype(jnp.bfloat16)
    key_rot = rotate(key_new.astype(jnp.float32), positions[..., None]).astype(jnp.bfloat16)
    attn_out = attend(query_rot, key_rot, value_new, cache_kv[0], lengths)
    new_kv = jnp.concatenate(
        [
            key_rot.reshape(local_requests, 2, KV_HEADS * HEAD_WIDTH),
            value_new.reshape(local_requests, 2, KV_HEADS * HEAD_WIDTH),
        ],
        axis=-1,
    )
    return (attn_out[None], new_kv[None])


SPLIT = 2
COLUMN_TILE = 256
MESH_ID = pl.DeviceIdType.MESH


def ring_to_tp(place, n):
    high = place // (n // 2)
    return (1 - high) * (2 * place) + high * (2 * (n - 1 - place) + 1)


def project_kernel(
    n,
    hidden_ref,
    gain_ref,
    weight_ref,
    up_ref,
    chip_ref,
    query_out,
    shared_out,
    normed,
    weight_buf,
    total,
    query_send,
    shared_send,
    up_all,
    sums_send,
    sums_all,
    reduce_send,
    reduce_recv,
    lowrank_all,
    weight_sem,
    ring_send,
    ring_recv,
    sums_send_sem,
    sums_recv_sem,
    up_send_sem,
    up_recv_sem,
    reduce_send_sem,
    reduce_recv_sem,
    spread_send_sem,
    spread_recv_sem,
    shared_send_sem,
    shared_recv_sem,
    query_send_sem,
    query_recv_sem,
):
    me = lax.axis_index("tp")
    rows, width = hidden_ref.shape
    own_rows = rows // n
    query_width = query_send.shape[1]
    shared_width = shared_send.shape[1]
    piece = rows // 2 // SPLIT

    def peer(d):
        return lax.rem(me + d, n)

    def source(d):
        return lax.rem(me + n - d, n)

    def rows_of(t):
        return pl.ds(pl.multiple_of(t * own_rows, own_rows), own_rows)

    def remote(src, dst, send_sem, recv_sem, target):
        return pltpu.make_async_remote_copy(
            src_ref=src,
            dst_ref=dst,
            send_sem=send_sem,
            recv_sem=recv_sem,
            device_id={"tp": target},
            device_id_type=MESH_ID,
        )

    barrier = pltpu.get_barrier_semaphore()
    for d in range(1, n):
        pl.semaphore_signal(barrier, inc=1, device_id={"tp": peer(d)}, device_id_type=MESH_ID)

    def weight_copy(block):
        return pltpu.make_async_copy(
            weight_ref.at[block], weight_buf.at[block], weight_sem.at[block]
        )

    for block in range(n):
        weight_copy(block).start()

    sums_send[...] = jnp.zeros_like(sums_send)
    for i in range(rows // 128):
        wide = hidden_ref[i * 128 : (i + 1) * 128, :].astype(jnp.float32)
        square = jnp.sum(wide * wide, axis=1, keepdims=True)
        sums_send[i : i + 1, :] = jnp.transpose(jnp.broadcast_to(square, (128, 128)))[0:1, :]
    sums_all[me] = sums_send[...]
    pl.semaphore_wait(barrier, n - 1)

    def sums_copy(d):
        return remote(
            sums_send, sums_all.at[me], sums_send_sem.at[d], sums_recv_sem.at[d], peer(d)
        )

    for d in range(1, n):
        sums_copy(d).start()
    for d in range(1, n):
        sums_copy(d).wait_recv()
    sums = sums_all[0]
    for t in range(1, n):
        sums = sums + sums_all[t]
    scale = lax.rsqrt(sums / (n * width) + norm_eps)
    for i in range(rows // 128):
        span = slice(i * 128, (i + 1) * 128)
        column = jnp.transpose(jnp.broadcast_to(scale[i : i + 1, :], (128, 128)))[:, 0:1]
        wide = hidden_ref[span, :].astype(jnp.float32)
        normed[me, span, :] = (wide * column * gain_ref[...]).astype(jnp.bfloat16)

    odd = lax.rem(me, 2)
    place = (1 - odd) * (me // 2) + odd * ((2 * n - 1 - me) // 2)
    right = ring_to_tp(lax.rem(place + 1, n), n)
    left = ring_to_tp(lax.rem(place + n - 1, n), n)

    def ring_part(direction, i):
        step, part = i // SPLIT, i % SPLIT
        if direction == 0:
            owner = ring_to_tp(lax.rem(place + n - step, n), n)
        else:
            owner = ring_to_tp(lax.rem(place + step, n), n)
        start = direction * (rows // 2) + part * piece
        if not isinstance(start, int):
            start = pl.multiple_of(start, piece)
        return owner, pl.ds(start, piece)

    def ring_copy(direction, i):
        owner, span = ring_part(direction, i)
        block = normed.at[owner, span]
        return remote(
            block,
            block,
            ring_send.at[direction, i],
            ring_recv.at[direction, i],
            left if direction else right,
        )

    def compute(i):
        parts = [ring_part(direction, i) for direction in range(2)]

        @pl.loop(0, total.shape[1] // COLUMN_TILE)
        def _(j):
            columns = pl.ds(pl.multiple_of(j * COLUMN_TILE, COLUMN_TILE), COLUMN_TILE)
            for owner, span in parts:
                total[span, columns] += jnp.dot(
                    normed[owner, span, :],
                    weight_buf[owner, :, columns],
                    preferred_element_type=jnp.float32,
                )

    for i in range(SPLIT):
        for direction in range(2):
            ring_copy(direction, i).start()

    def up_copy(d):
        return remote(
            up_ref.at[peer(d)], up_all.at[me], up_send_sem.at[d], up_recv_sem.at[d], peer(d)
        )

    for d in range(1, n):
        up_copy(d).start()
    up_all[me] = up_ref[me]
    total[...] = jnp.zeros_like(total)
    for block in range(n):
        weight_copy(block).wait()

    def first(i, _):
        compute(i)
        return 0

    lax.fori_loop(0, SPLIT, first, 0)

    def middle(i, _):
        for direction in range(2):
            ring_copy(direction, i - SPLIT).wait_recv()
            ring_copy(direction, i).start()
        compute(i)
        return 0

    lax.fori_loop(SPLIT, (n - 1) * SPLIT, middle, 0)

    def last(i, _):
        for direction in range(2):
            ring_copy(direction, i - SPLIT).wait_recv()
        compute(i)
        return 0

    lax.fori_loop((n - 1) * SPLIT, n * SPLIT, last, 0)

    low_column = query_width + shared_width
    for t in range(n):
        span = slice(t * own_rows, (t + 1) * own_rows)
        low = total[span, low_column : low_column + 128]
        reduce_send[span, :] = jnp.where(chip_ref[span, :] == me, low, 0.0).astype(jnp.bfloat16)

    def reduce_copy(d):
        return remote(
            reduce_send.at[rows_of(peer(d))],
            reduce_recv.at[me],
            reduce_send_sem.at[d],
            reduce_recv_sem.at[d],
            peer(d),
        )

    for d in range(1, n):
        reduce_copy(d).start()
    reduce_recv[me] = reduce_send[rows_of(me), :]

    shared_send[...] = total[:, query_width:low_column].astype(jnp.bfloat16)

    def shared_copy(d):
        return remote(
            shared_send.at[rows_of(peer(d))],
            shared_out.at[me],
            shared_send_sem.at[d],
            shared_recv_sem.at[d],
            peer(d),
        )

    for d in range(1, n):
        reduce_copy(d).wait_recv()
    low = reduce_recv[0].astype(jnp.float32)
    for t in range(1, n):
        low = low + reduce_recv[t].astype(jnp.float32)
    lowrank_all[me] = low.astype(jnp.bfloat16)

    def spread_copy(d):
        return remote(
            lowrank_all.at[me],
            lowrank_all.at[me],
            spread_send_sem.at[d],
            spread_recv_sem.at[d],
            peer(d),
        )

    for d in range(1, n):
        spread_copy(d).start()
    for d in range(1, n):
        shared_copy(d).start()
    shared_out[me] = shared_send[rows_of(me), :]
    for d in range(1, n):
        up_copy(d).wait_recv()
    for d in range(1, n):
        spread_copy(d).wait_recv()

    def mixed(t):
        low = lowrank_all[t].astype(jnp.float32)
        chip = chip_ref[rows_of(t), :]
        tiles = []
        for pair in range(n // 2):
            even_part = jnp.where(chip == 2 * pair, low, 0.0)
            odd_part = jnp.where(chip == 2 * pair + 1, low, 0.0)
            tiles.append((even_part + pltpu.roll(odd_part, RANK, 1)).astype(jnp.bfloat16))
        spread = jnp.concatenate(tiles, axis=1)
        up = up_all[...].reshape(n * RANK, query_width)
        delta = jnp.dot(spread, up, preferred_element_type=jnp.float32)
        query = total[rows_of(t), 0:query_width]
        return (query + adapter_scale * delta).astype(jnp.bfloat16)

    def query_copy(d):
        return remote(
            query_send.at[rows_of(peer(d))],
            query_out.at[me],
            query_send_sem.at[d],
            query_recv_sem.at[d],
            peer(d),
        )

    def send_query(d, _):
        query_send[rows_of(peer(d)), :] = mixed(peer(d))
        query_copy(d).start()
        return 0

    lax.fori_loop(1, n, send_query, 0)
    query_out[me] = mixed(me)

    for d in range(1, n):
        shared_copy(d).wait_recv()
        query_copy(d).wait_recv()

    def drain(i, _):
        for direction in range(2):
            ring_copy(direction, i).wait_send()
        return 0

    lax.fori_loop(0, (n - 1) * SPLIT, drain, 0)
    for d in range(1, n):
        sums_copy(d).wait_send()
        up_copy(d).wait_send()
        reduce_copy(d).wait_send()
        spread_copy(d).wait_send()
        shared_copy(d).wait_send()
        query_copy(d).wait_send()


def project_rows(n, hidden, gain, weight, up, chip):
    rows, width = hidden.shape
    columns = weight.shape[2]
    own_rows = rows // n
    query_width = up.shape[2]
    shared_width = query_width // HEAD_WIDTH * KEY_VALUE_SHARE
    dma = pltpu.SemaphoreType.DMA
    vmem = pl.BlockSpec(memory_space=pltpu.VMEM)
    bf16, f32 = jnp.bfloat16, jnp.float32
    return pl.pallas_call(
        functools.partial(project_kernel, n),
        out_shape=(
            jax.ShapeDtypeStruct((n, own_rows, query_width), bf16),
            jax.ShapeDtypeStruct((n, own_rows, shared_width), bf16),
        ),
        in_specs=[vmem, vmem, pl.BlockSpec(memory_space=pl.ANY), vmem, vmem],
        out_specs=(vmem, vmem),
        scratch_shapes=[
            pltpu.VMEM((n, rows, width), bf16),
            pltpu.VMEM((n, width, columns), bf16),
            pltpu.VMEM((rows, columns), f32),
            pltpu.VMEM((rows, query_width), bf16),
            pltpu.VMEM((rows, shared_width), bf16),
            pltpu.VMEM((n, RANK, query_width), bf16),
            pltpu.VMEM((8, 128), f32),
            pltpu.VMEM((n, 8, 128), f32),
            pltpu.VMEM((rows, 128), bf16),
            pltpu.VMEM((n, own_rows, 128), bf16),
            pltpu.VMEM((n, own_rows, 128), bf16),
            dma((n,)),
            dma((2, (n - 1) * SPLIT)),
            dma((2, (n - 1) * SPLIT)),
        ]
        + [dma((n,))] * 12,
        compiler_params=pltpu.CompilerParams(
            collective_id=0, has_side_effects=True, vmem_limit_bytes=60 * 1024 * 1024
        ),
        cost_estimate=pl.CostEstimate(
            flops=2 * rows * width * n * columns,
            bytes_accessed=2 * n * width * columns,
            transcendentals=0,
        ),
    )(hidden, gain, weight, up, chip)


def attend_kernel(
    length_ref, query_ref, cos_ref, sin_ref, new_ref, cache_ref, out_ref
):
    count = query_ref.shape[0]
    lanes = KV_HEADS * HEAD_WIDTH
    pad = new_ref.shape[1]
    first = pl.program_id(0) * count
    factor = HEAD_WIDTH ** (-0.5)
    row = lax.broadcasted_iota(jnp.int32, (2 * HEADS, lanes), 0)
    lane = lax.broadcasted_iota(jnp.int32, (2 * HEADS, lanes), 1)
    own = (row // GROUP) % KV_HEADS == lane // HEAD_WIDTH
    key_at = lax.broadcasted_iota(jnp.int32, (2 * HEADS, CACHE), 1)
    new_at = lax.broadcasted_iota(jnp.int32, (2 * HEADS, pad), 1)
    new_limit = lax.broadcasted_iota(jnp.int32, (2 * HEADS, pad), 0) // HEADS
    across = (((1,), (1,)), ((), ()))
    for b in range(count):
        query = query_ref[b].astype(jnp.float32)
        turned = pltpu.roll(query, HEAD_WIDTH // 2, 1)
        rotated = jnp.concatenate(
            [
                query[p * HEADS : (p + 1) * HEADS] * cos_ref[b, p : p + 1, :]
                + turned[p * HEADS : (p + 1) * HEADS] * sin_ref[b, p : p + 1, :]
                for p in range(2)
            ],
            axis=0,
        ).astype(jnp.bfloat16)
        wide = jnp.concatenate([rotated] * KV_HEADS, axis=1)
        wide = jnp.where(own, wide, jnp.zeros((), jnp.bfloat16))
        old = (
            lax.dot_general(
                wide, cache_ref[b, :, 0:lanes], across, preferred_element_type=jnp.float32
            )
            * factor
        )
        new = (
            lax.dot_general(
                wide, new_ref[b, :, 0:lanes], across, preferred_element_type=jnp.float32
            )
            * factor
        )
        old = jnp.where(key_at < length_ref[first + b], old, masked_out)
        new = jnp.where(new_at <= new_limit, new, masked_out)
        highest = jnp.maximum(
            jnp.max(old, axis=1, keepdims=True), jnp.max(new, axis=1, keepdims=True)
        )
        old_exp = jnp.exp(old - highest)
        new_exp = jnp.exp(new - highest)
        denominator = jnp.sum(old_exp, axis=1, keepdims=True) + jnp.sum(
            new_exp, axis=1, keepdims=True
        )
        old_weights = (old_exp / denominator).astype(jnp.bfloat16)
        new_weights = (new_exp / denominator).astype(jnp.bfloat16)
        mixture = jnp.dot(
            old_weights, cache_ref[b, :, lanes:], preferred_element_type=jnp.float32
        ) + jnp.dot(new_weights, new_ref[b, :, lanes:], preferred_element_type=jnp.float32)
        pieces = []
        for p in range(2):
            for g in range(KV_HEADS):
                start = p * HEADS + g * GROUP
                pieces.append(
                    mixture[start : start + GROUP, g * HEAD_WIDTH : (g + 1) * HEAD_WIDTH]
                )
        out_ref[b] = jnp.concatenate(pieces, axis=0).astype(jnp.bfloat16)


def attend_rows(lengths, query, cosine, sine, new, cache):
    requests = query.shape[0]
    block = 4

    def spec(*shape):
        return pl.BlockSpec((block,) + shape, lambda i: (i,) + (0,) * len(shape))

    return pl.pallas_call(
        attend_kernel,
        grid=(requests // block,),
        out_shape=jax.ShapeDtypeStruct((requests, 2 * HEADS, HEAD_WIDTH), jnp.bfloat16),
        in_specs=[
            pl.BlockSpec(memory_space=pltpu.SMEM),
            spec(2 * HEADS, HEAD_WIDTH),
            spec(2, HEAD_WIDTH),
            spec(2, HEAD_WIDTH),
            spec(new.shape[1], new.shape[2]),
            spec(CACHE, cache.shape[2]),
        ],
        out_specs=spec(2 * HEADS, HEAD_WIDTH),
        compiler_params=pltpu.CompilerParams(vmem_limit_bytes=32 * 1024 * 1024),
        cost_estimate=pl.CostEstimate(
            flops=4 * requests * 2 * HEADS * HEAD_WIDTH * CACHE * KV_HEADS,
            bytes_accessed=2 * requests * CACHE * cache.shape[2],
            transcendentals=requests * 2 * HEADS * CACHE,
        ),
    )(lengths, query, cosine, sine, new, cache)


def ring_body(
    tp_count,
    dp_count,
    hidden,
    norm_gain,
    w_qkv,
    adapter_store,
    adapter_home,
    slot_adapter,
    request_slot,
    cache_kv,
    cache_len,
):
    tp_index = lax.axis_index("tp")
    dp_index = lax.axis_index("dp")
    requests = hidden.shape[1]
    local_width = hidden.shape[3]
    device_heads = w_qkv.shape[1]
    local_requests = requests // tp_count
    rows = requests * 2
    column_start = tp_index * local_width

    per_chip = dp_count * ADAPT_DEV
    stored_rows = adapter_home[slot_adapter]
    slot_chip = stored_rows // per_chip
    within = jnp.sum(jnp.where(slot_chip == tp_index, stored_rows % per_chip, 0), axis=1)
    holder, local_slot = within // ADAPT_DEV, within % ADAPT_DEV
    other = 1 - dp_index
    mine = lax.dynamic_index_in_dim(adapter_store, local_slot[dp_index], 0, keepdims=False)
    theirs = lax.dynamic_index_in_dim(adapter_store, local_slot[other], 0, keepdims=False)
    swapped = lax.ppermute(theirs, "dp", [(0, 1), (1, 0)])
    adapter = jnp.where(holder[dp_index] == dp_index, mine, swapped)
    down = adapter[:, :RANK]
    up = jnp.transpose(
        adapter[:, RANK:].reshape(tp_count, local_width, RANK), (0, 2, 1)
    )
    row_chip = jnp.repeat(slot_chip[dp_index][request_slot[0]], 2)
    chip = jnp.broadcast_to(row_chip[:, None], (rows, 128))

    query_width = device_heads * HEAD_WIDTH
    shared_width = device_heads * KEY_VALUE_SHARE
    used = query_width + shared_width + RANK
    columns = -(-used // COLUMN_TILE) * COLUMN_TILE
    weight = jnp.concatenate(
        [
            w_qkv[:, :, :HEAD_WIDTH].reshape(D, query_width),
            w_qkv[:, :, HEAD_WIDTH:].reshape(D, shared_width),
            down,
            jnp.zeros((D, columns - used), jnp.bfloat16),
        ],
        axis=1,
    ).reshape(tp_count, local_width, columns)
    gain = lax.dynamic_slice_in_dim(norm_gain, column_start, local_width, 0)
    gain = gain.astype(jnp.float32)[None, :]
    query, shared = project_rows(
        tp_count, hidden[0].reshape(rows, local_width), gain, weight, up, chip
    )
    query = query.reshape(tp_count, local_requests, 2, device_heads, HEAD_WIDTH)
    query = jnp.transpose(query, (1, 2, 0, 3, 4)).reshape(local_requests, 2 * HEADS, HEAD_WIDTH)
    shared = jnp.transpose(
        shared.reshape(tp_count, local_requests, 2, shared_width), (1, 2, 0, 3)
    ).reshape(local_requests, 2, HEADS * KEY_VALUE_SHARE)
    half = KV_HEADS * HEAD_WIDTH
    lengths = cache_len[0]
    positions = (lengths[:, None] + jnp.arange(2, dtype=jnp.int32)[None, :]).astype(jnp.float32)
    counter = jnp.arange(HEAD_WIDTH // 2, dtype=jnp.float32)
    inverse_freq = rope_base ** (-2.0 * counter / HEAD_WIDTH)
    angles = positions[..., None] * inverse_freq
    cosine, sine = jnp.cos(angles), jnp.sin(angles)
    cos_wide = jnp.concatenate([cosine, cosine], axis=-1)
    sin_wide = jnp.concatenate([-sine, sine], axis=-1)
    key_new = shared[..., :half].reshape(local_requests, 2, KV_HEADS, HEAD_WIDTH)
    key_wide = key_new.astype(jnp.float32)
    key_turned = jnp.roll(key_wide, HEAD_WIDTH // 2, axis=-1)
    key_rot = (
        key_wide * cos_wide[:, :, None, :] + key_turned * sin_wide[:, :, None, :]
    ).astype(jnp.bfloat16)
    new_kv = jnp.concatenate(
        [key_rot.reshape(local_requests, 2, half), shared[..., half:]], axis=-1
    )
    new_padded = jnp.pad(new_kv, ((0, 0), (0, 14), (0, 0)))
    attended = attend_rows(lengths, query, cos_wide, sin_wide, new_padded, cache_kv[0])
    attn_out = attended.reshape(local_requests, 2, HEADS * HEAD_WIDTH)
    return (attn_out[None], new_kv[None])


def body(tp_count, dp_count, hidden, norm_gain, w_qkv, *rest):
    rows = hidden.shape[1] * 2
    shared_width = w_qkv.shape[1] * KEY_VALUE_SHARE
    fits = (
        dp_count == 2
        and tp_count % 2 == 0
        and rows % (tp_count * 16) == 0
        and rows % 128 == 0
        and rows <= 1024
        and hidden.shape[3] % 128 == 0
        and shared_width % 128 == 0
        and (rows // 2) % (SPLIT * 16) == 0
    )
    if fits:
        return ring_body(tp_count, dp_count, hidden, norm_gain, w_qkv, *rest)
    return plain_body(hidden, norm_gain, w_qkv, *rest)


def solution(mesh):
    placed = (
        P(("group", "dp"), None, None, "tp"),
        P(),
        P(None, "tp", None),
        P(("group", "tp", "dp"), None, None),
        P("group"),
        P("group", None),
        P(("group", "dp"), None),
        P(("group", "dp"), "tp", None, None),
        P(("group", "dp"), "tp"),
    )
    return jax.shard_map(
        functools.partial(body, mesh.shape["tp"], mesh.shape["dp"]),
        mesh=mesh,
        in_specs=placed,
        out_specs=(P(("group", "dp"), "tp", None, None), P(("group", "dp"), "tp", None, None)),
        check_vma=False,
    )
```

```python
import functools

import jax
import jax.numpy as jnp
from jax import lax
from jax.experimental import pallas as pl
from jax.experimental.pallas import tpu as pltpu
from jax.sharding import PartitionSpec as P

D = 8192
HEADS = 64
KV_HEADS = 8
HEAD_WIDTH = 128
RANK = 64
CACHE = 128
ADAPT_DEV = 3
KEY_VALUE_SHARE = 32
GROUP = 8


adapter_scale = 0.0625
rope_base = 500000.0
norm_eps = 1e-05
masked_out = -1e30


def rotate(vectors, positions):
    halfway = vectors.shape[-1] // 2
    counter = jnp.arange(halfway, dtype=jnp.float32)
    inverse_freq = rope_base ** (-2.0 * counter / vectors.shape[-1])
    angles = positions[..., None] * inverse_freq
    cosine = jnp.cos(angles)
    sine_part = jnp.sin(angles)
    leading = vectors[..., :halfway]
    trailing = vectors[..., halfway:]
    return jnp.concatenate(
        [leading * cosine - trailing * sine_part, trailing * cosine + leading * sine_part], axis=-1
    )


def attend(query_rot, key_rot, value_new, cache_block, length_block):
    batch_count = query_rot.shape[0]
    grouped = query_rot.reshape(batch_count, 2, KV_HEADS, GROUP, HEAD_WIDTH)
    cache_keys = cache_block[:, :, : KV_HEADS * HEAD_WIDTH].reshape(
        batch_count, CACHE, KV_HEADS, HEAD_WIDTH
    )
    cache_values = cache_block[:, :, KV_HEADS * HEAD_WIDTH :].reshape(
        batch_count, CACHE, KV_HEADS, HEAD_WIDTH
    )
    factor = HEAD_WIDTH ** (-0.5)
    old_scores = (
        jnp.einsum("rpgjc,rlgc->rpgjl", grouped, cache_keys, preferred_element_type=jnp.float32)
        * factor
    )
    new_scores = (
        jnp.einsum("rpgjc,rngc->rpgjn", grouped, key_rot, preferred_element_type=jnp.float32)
        * factor
    )
    old_valid = jnp.arange(CACHE, dtype=jnp.int32)[None, :] < length_block[:, None]
    new_valid = jnp.arange(2, dtype=jnp.int32)[None, :] <= jnp.arange(2, dtype=jnp.int32)[:, None]
    old_scores = jnp.where(old_valid[:, None, None, None, :], old_scores, masked_out)
    new_scores = jnp.where(new_valid[None, :, None, None, :], new_scores, masked_out)
    highest = jnp.maximum(jnp.max(old_scores, axis=-1), jnp.max(new_scores, axis=-1))[..., None]
    old_exp = jnp.exp(old_scores - highest)
    new_exp = jnp.exp(new_scores - highest)
    denominator = jnp.sum(old_exp, axis=-1, keepdims=True) + jnp.sum(
        new_exp, axis=-1, keepdims=True
    )
    old_weights = (old_exp / denominator).astype(jnp.bfloat16)
    new_weights = (new_exp / denominator).astype(jnp.bfloat16)
    mixture = jnp.einsum(
        "rpgjl,rlgc->rpgjc", old_weights, cache_values, preferred_element_type=jnp.float32
    )
    mixture = mixture + jnp.einsum(
        "rpgjn,rngc->rpgjc", new_weights, value_new, preferred_element_type=jnp.float32
    )
    return mixture.astype(jnp.bfloat16).reshape(batch_count, 2, HEADS * HEAD_WIDTH)


def slot_delta(slot_slices, local_normed, chosen, count_of_rows, slot_count, local_width):
    down_matrix = jnp.transpose(slot_slices[:, :, :RANK], (1, 0, 2)).reshape(
        local_width, slot_count * RANK
    )
    partial_rank = jnp.dot(local_normed, down_matrix, preferred_element_type=jnp.float32).reshape(
        count_of_rows, slot_count, RANK
    )
    partial_rank = jnp.sum(jnp.where(chosen[:, :, None], partial_rank, 0.0), axis=1)
    lowrank = lax.psum(partial_rank, "tp").astype(jnp.bfloat16)
    spread = jnp.where(
        chosen[:, :, None], lowrank[:, None, :], jnp.zeros((), jnp.bfloat16)
    ).reshape(count_of_rows, slot_count * RANK)
    up_matrix = jnp.transpose(slot_slices[:, :, RANK:], (0, 2, 1)).reshape(
        slot_count * RANK, local_width
    )
    return jnp.dot(spread, up_matrix, preferred_element_type=jnp.float32)


def plain_body(
    hidden,
    norm_gain,
    w_qkv,
    adapter_store,
    adapter_home,
    slot_adapter,
    request_slot,
    cache_kv,
    cache_len,
):
    tp_count = lax.axis_size("tp")
    dp_count = lax.axis_size("dp")
    tp_index = lax.axis_index("tp")
    dp_index = lax.axis_index("dp")
    requests = hidden.shape[1]
    local_width = hidden.shape[3]
    device_heads = w_qkv.shape[1]
    slot_count = slot_adapter.shape[1]
    count_of_rows = requests * 2
    flat_rows = hidden[0].reshape(count_of_rows, local_width)
    gain_wide = norm_gain.astype(jnp.float32)
    weights = w_qkv.reshape(D, device_heads * (HEAD_WIDTH + KEY_VALUE_SHARE))
    column_start = tp_index * local_width
    stored_rows = adapter_home[slot_adapter]
    block_rows = lax.dynamic_index_in_dim(stored_rows, dp_index, 0, keepdims=False)
    device_index = tp_index * dp_count + dp_index
    offsets = stored_rows - device_index * ADAPT_DEV
    local_slots = jnp.arange(ADAPT_DEV, dtype=jnp.int32)
    selector = jnp.any(offsets[:, :, None] == local_slots[None, None, :], axis=1).astype(
        jnp.bfloat16
    )
    row_slot = jnp.repeat(request_slot[0], 2)
    chosen = row_slot[:, None] == jnp.arange(slot_count, dtype=jnp.int32)[None, :]
    gathered = lax.all_gather(flat_rows, "tp", axis=1, tiled=True)
    widened = gathered.astype(jnp.float32)
    mean_square = jnp.mean(widened * widened, axis=1, keepdims=True)
    normed = (widened * lax.rsqrt(mean_square + norm_eps) * gain_wide).astype(jnp.bfloat16)
    local_normed = lax.dynamic_slice_in_dim(normed, column_start, local_width, 1)
    projected_whole = jnp.dot(normed, weights, preferred_element_type=jnp.float32)
    pieces = adapter_store.reshape(ADAPT_DEV, tp_count, local_width, 2 * RANK)
    outgoing = jnp.einsum(
        "bm,mtlk->tblk", selector, pieces, preferred_element_type=jnp.float32
    ).astype(jnp.bfloat16)
    outgoing = outgoing.reshape(tp_count * dp_count, local_width, 2 * RANK)
    incoming = lax.all_to_all(outgoing, ("tp", "dp"), split_axis=0, concat_axis=0, tiled=True)
    slot_slices = jnp.take(incoming, block_rows // ADAPT_DEV, axis=0)
    delta_query = slot_delta(
        slot_slices, local_normed, chosen, count_of_rows, slot_count, local_width
    )
    delta_padded_rows = jnp.pad(
        delta_query.reshape(count_of_rows, device_heads, HEAD_WIDTH),
        ((0, 0), (0, 0), (0, KEY_VALUE_SHARE)),
    )
    packed_columns = (
        projected_whole.reshape(count_of_rows, device_heads, HEAD_WIDTH + KEY_VALUE_SHARE)
        + adapter_scale * delta_padded_rows
    ).astype(jnp.bfloat16)
    packed_columns = packed_columns.reshape(requests, 2, device_heads, HEAD_WIDTH + KEY_VALUE_SHARE)
    arrived_heads = lax.all_to_all(packed_columns, "tp", split_axis=0, concat_axis=2, tiled=True)
    local_requests = arrived_heads.shape[0]
    query_part = arrived_heads[..., :HEAD_WIDTH]
    shared = arrived_heads[..., HEAD_WIDTH:].reshape(local_requests, 2, HEADS * KEY_VALUE_SHARE)
    key_new = shared[..., : KV_HEADS * HEAD_WIDTH].reshape(local_requests, 2, KV_HEADS, HEAD_WIDTH)
    value_new = shared[..., KV_HEADS * HEAD_WIDTH :].reshape(
        local_requests, 2, KV_HEADS, HEAD_WIDTH
    )
    lengths = cache_len[0]
    positions = (lengths[:, None] + jnp.arange(2, dtype=jnp.int32)[None, :]).astype(jnp.float32)
    query_rot = rotate(query_part.astype(jnp.float32), positions[..., None]).astype(jnp.bfloat16)
    key_rot = rotate(key_new.astype(jnp.float32), positions[..., None]).astype(jnp.bfloat16)
    attn_out = attend(query_rot, key_rot, value_new, cache_kv[0], lengths)
    new_kv = jnp.concatenate(
        [
            key_rot.reshape(local_requests, 2, KV_HEADS * HEAD_WIDTH),
            value_new.reshape(local_requests, 2, KV_HEADS * HEAD_WIDTH),
        ],
        axis=-1,
    )
    return (attn_out[None], new_kv[None])


SPLIT = 2
COLUMN_TILE = 256
MESH_ID = pl.DeviceIdType.MESH


def ring_to_tp(place, n):
    high = place // (n // 2)
    return (1 - high) * (2 * place) + high * (2 * (n - 1 - place) + 1)


def project_kernel(
    n,
    hidden_ref,
    gain_ref,
    weight_ref,
    adapter_ref,
    chip_ref,
    query_out,
    shared_out,
    normed,
    weight_buf,
    total,
    query_send,
    shared_send,
    up_all,
    sums_send,
    sums_all,
    reduce_send,
    reduce_recv,
    lowrank_all,
    weight_sem,
    ring_send,
    ring_recv,
    sums_send_sem,
    sums_recv_sem,
    up_send_sem,
    up_recv_sem,
    reduce_send_sem,
    reduce_recv_sem,
    spread_send_sem,
    spread_recv_sem,
    shared_send_sem,
    shared_recv_sem,
    query_send_sem,
    query_recv_sem,
):
    me = lax.axis_index("tp")
    rows, width = hidden_ref.shape
    own_rows = rows // n
    query_width = query_send.shape[1]
    shared_width = shared_send.shape[1]
    piece = rows // 2 // SPLIT

    def peer(d):
        return lax.rem(me + d, n)

    def source(d):
        return lax.rem(me + n - d, n)

    def rows_of(t):
        return pl.ds(pl.multiple_of(t * own_rows, own_rows), own_rows)

    def remote(src, dst, send_sem, recv_sem, target):
        return pltpu.make_async_remote_copy(
            src_ref=src,
            dst_ref=dst,
            send_sem=send_sem,
            recv_sem=recv_sem,
            device_id={"tp": target},
            device_id_type=MESH_ID,
        )

    barrier = pltpu.get_barrier_semaphore()
    for d in range(1, n):
        pl.semaphore_signal(barrier, inc=1, device_id={"tp": peer(d)}, device_id_type=MESH_ID)

    heads = weight_ref.shape[0]
    low_column = query_width + shared_width
    adapter_copy = pltpu.make_async_copy(
        adapter_ref, weight_buf.at[pl.ds(low_column, 2 * RANK)], weight_sem.at[2 * heads]
    )
    adapter_copy.start()

    def weight_copies(head):
        return (
            pltpu.make_async_copy(
                weight_ref.at[head, pl.ds(0, HEAD_WIDTH)],
                weight_buf.at[pl.ds(head * HEAD_WIDTH, HEAD_WIDTH)],
                weight_sem.at[2 * head],
            ),
            pltpu.make_async_copy(
                weight_ref.at[head, pl.ds(HEAD_WIDTH, KEY_VALUE_SHARE)],
                weight_buf.at[pl.ds(query_width + head * KEY_VALUE_SHARE, KEY_VALUE_SHARE)],
                weight_sem.at[2 * head + 1],
            ),
        )

    for head in range(heads):
        for copy in weight_copies(head):
            copy.start()

    sums_send[...] = jnp.zeros_like(sums_send)
    for i in range(rows // 128):
        wide = hidden_ref[i * 128 : (i + 1) * 128, :].astype(jnp.float32)
        square = jnp.sum(wide * wide, axis=1, keepdims=True)
        sums_send[i : i + 1, :] = jnp.transpose(jnp.broadcast_to(square, (128, 128)))[0:1, :]
    sums_all[me] = sums_send[...]
    pl.semaphore_wait(barrier, n - 1)

    def sums_copy(d):
        return remote(
            sums_send, sums_all.at[me], sums_send_sem.at[d], sums_recv_sem.at[d], peer(d)
        )

    for d in range(1, n):
        sums_copy(d).start()
    for d in range(1, n):
        sums_copy(d).wait_recv()
    sums = sums_all[0]
    for t in range(1, n):
        sums = sums + sums_all[t]
    scale = lax.rsqrt(sums / (n * width) + norm_eps)
    for i in range(rows // 128):
        span = slice(i * 128, (i + 1) * 128)
        column = jnp.transpose(jnp.broadcast_to(scale[i : i + 1, :], (128, 128)))[:, 0:1]
        wide = hidden_ref[span, :].astype(jnp.float32)
        normed[me, span, :] = (wide * column * gain_ref[...]).astype(jnp.bfloat16)

    odd = lax.rem(me, 2)
    place = (1 - odd) * (me // 2) + odd * ((2 * n - 1 - me) // 2)
    right = ring_to_tp(lax.rem(place + 1, n), n)
    left = ring_to_tp(lax.rem(place + n - 1, n), n)

    def ring_part(direction, i):
        step, part = i // SPLIT, i % SPLIT
        if direction == 0:
            owner = ring_to_tp(lax.rem(place + n - step, n), n)
        else:
            owner = ring_to_tp(lax.rem(place + step, n), n)
        start = direction * (rows // 2) + part * piece
        if not isinstance(start, int):
            start = pl.multiple_of(start, piece)
        return owner, pl.ds(start, piece)

    def ring_copy(direction, i):
        owner, span = ring_part(direction, i)
        block = normed.at[owner, span]
        return remote(
            block,
            block,
            ring_send.at[direction, i],
            ring_recv.at[direction, i],
            left if direction else right,
        )

    def compute(i):
        parts = [ring_part(direction, i) for direction in range(2)]

        def add(columns):
            for owner, span in parts:
                features = pl.ds(pl.multiple_of(owner * width, width), width)
                total[span, columns] += lax.dot_general(
                    normed[owner, span, :],
                    weight_buf[columns, features],
                    (((1,), (1,)), ((), ())),
                    preferred_element_type=jnp.float32,
                )

        @pl.loop(0, low_column // COLUMN_TILE)
        def _(j):
            add(pl.ds(pl.multiple_of(j * COLUMN_TILE, COLUMN_TILE), COLUMN_TILE))

        add(pl.ds(low_column, 2 * RANK))

    for i in range(SPLIT):
        for direction in range(2):
            ring_copy(direction, i).start()

    def up_slice(t):
        features = pl.ds(pl.multiple_of(t * width, width), width)
        return weight_buf.at[pl.ds(low_column + RANK, RANK), features]

    def up_copy(d):
        return remote(
            up_slice(peer(d)), up_all.at[me], up_send_sem.at[d], up_recv_sem.at[d], peer(d)
        )

    adapter_copy.wait()
    for d in range(1, n):
        up_copy(d).start()
    up_all[me] = up_slice(me)[...]
    total[...] = jnp.zeros_like(total)
    for head in range(heads):
        for copy in weight_copies(head):
            copy.wait()

    def first(i, _):
        compute(i)
        return 0

    lax.fori_loop(0, SPLIT, first, 0)

    def middle(i, _):
        for direction in range(2):
            ring_copy(direction, i - SPLIT).wait_recv()
            ring_copy(direction, i).start()
        compute(i)
        return 0

    lax.fori_loop(SPLIT, (n - 1) * SPLIT, middle, 0)

    def last(i, _):
        for direction in range(2):
            ring_copy(direction, i - SPLIT).wait_recv()
        compute(i)
        return 0

    lax.fori_loop((n - 1) * SPLIT, n * SPLIT, last, 0)

    lane = lax.broadcasted_iota(jnp.int32, (own_rows, 128), 1)
    for t in range(n):
        span = slice(t * own_rows, (t + 1) * own_rows)
        low = total[span, low_column : low_column + 128]
        reduce_send[span, :] = jnp.where(
            (chip_ref[span, :] == me) & (lane < RANK), low, 0.0
        ).astype(jnp.bfloat16)

    def reduce_copy(d):
        return remote(
            reduce_send.at[rows_of(peer(d))],
            reduce_recv.at[me],
            reduce_send_sem.at[d],
            reduce_recv_sem.at[d],
            peer(d),
        )

    for d in range(1, n):
        reduce_copy(d).start()
    reduce_recv[me] = reduce_send[rows_of(me), :]

    shared_send[...] = total[:, query_width:low_column].astype(jnp.bfloat16)

    def shared_copy(d):
        return remote(
            shared_send.at[rows_of(peer(d))],
            shared_out.at[me],
            shared_send_sem.at[d],
            shared_recv_sem.at[d],
            peer(d),
        )

    for d in range(1, n):
        reduce_copy(d).wait_recv()
    low = reduce_recv[0].astype(jnp.float32)
    for t in range(1, n):
        low = low + reduce_recv[t].astype(jnp.float32)
    lowrank_all[me] = low.astype(jnp.bfloat16)

    def spread_copy(d):
        return remote(
            lowrank_all.at[me],
            lowrank_all.at[me],
            spread_send_sem.at[d],
            spread_recv_sem.at[d],
            peer(d),
        )

    for d in range(1, n):
        spread_copy(d).start()
    for d in range(1, n):
        shared_copy(d).start()
    shared_out[me] = shared_send[rows_of(me), :]
    for d in range(1, n):
        up_copy(d).wait_recv()
    for d in range(1, n):
        spread_copy(d).wait_recv()

    def mixed(t):
        low = lowrank_all[t].astype(jnp.float32)
        chip = chip_ref[rows_of(t), :]
        tiles = []
        for pair in range(n // 2):
            even_part = jnp.where(chip == 2 * pair, low, 0.0)
            odd_part = jnp.where(chip == 2 * pair + 1, low, 0.0)
            tiles.append((even_part + pltpu.roll(odd_part, RANK, 1)).astype(jnp.bfloat16))
        spread = jnp.concatenate(tiles, axis=1)
        up = up_all[...].reshape(n * RANK, query_width)
        delta = jnp.dot(spread, up, preferred_element_type=jnp.float32)
        query = total[rows_of(t), 0:query_width]
        return (query + adapter_scale * delta).astype(jnp.bfloat16)

    def query_copy(d):
        return remote(
            query_send.at[rows_of(peer(d))],
            query_out.at[me],
            query_send_sem.at[d],
            query_recv_sem.at[d],
            peer(d),
        )

    def send_query(d, _):
        query_send[rows_of(peer(d)), :] = mixed(peer(d))
        query_copy(d).start()
        return 0

    lax.fori_loop(1, n, send_query, 0)
    query_out[me] = mixed(me)

    for d in range(1, n):
        shared_copy(d).wait_recv()
        query_copy(d).wait_recv()

    def drain(i, _):
        for direction in range(2):
            ring_copy(direction, i).wait_send()
        return 0

    lax.fori_loop(0, (n - 1) * SPLIT, drain, 0)
    for d in range(1, n):
        sums_copy(d).wait_send()
        up_copy(d).wait_send()
        reduce_copy(d).wait_send()
        spread_copy(d).wait_send()
        shared_copy(d).wait_send()
        query_copy(d).wait_send()


def project_rows(n, hidden, gain, weight, adapter, chip):
    rows, width = hidden.shape
    heads = weight.shape[0]
    own_rows = rows // n
    query_width = heads * HEAD_WIDTH
    shared_width = heads * KEY_VALUE_SHARE
    columns = query_width + shared_width + 2 * RANK
    dma = pltpu.SemaphoreType.DMA
    vmem = pl.BlockSpec(memory_space=pltpu.VMEM)
    hbm = pl.BlockSpec(memory_space=pl.ANY)
    bf16, f32 = jnp.bfloat16, jnp.float32
    return pl.pallas_call(
        functools.partial(project_kernel, n),
        out_shape=(
            jax.ShapeDtypeStruct((n, own_rows, query_width), bf16),
            jax.ShapeDtypeStruct((n, own_rows, shared_width), bf16),
        ),
        in_specs=[vmem, vmem, hbm, hbm, vmem],
        out_specs=(vmem, vmem),
        scratch_shapes=[
            pltpu.VMEM((n, rows, width), bf16),
            pltpu.VMEM((columns, n * width), bf16),
            pltpu.VMEM((rows, columns), f32),
            pltpu.VMEM((rows, query_width), bf16),
            pltpu.VMEM((rows, shared_width), bf16),
            pltpu.VMEM((n, RANK, query_width), bf16),
            pltpu.VMEM((8, 128), f32),
            pltpu.VMEM((n, 8, 128), f32),
            pltpu.VMEM((rows, 128), bf16),
            pltpu.VMEM((n, own_rows, 128), bf16),
            pltpu.VMEM((n, own_rows, 128), bf16),
            dma((2 * heads + 1,)),
            dma((2, (n - 1) * SPLIT)),
            dma((2, (n - 1) * SPLIT)),
        ]
        + [dma((n,))] * 12,
        compiler_params=pltpu.CompilerParams(
            collective_id=0, has_side_effects=True, vmem_limit_bytes=60 * 1024 * 1024
        ),
        cost_estimate=pl.CostEstimate(
            flops=2 * rows * width * n * columns,
            bytes_accessed=2 * n * width * columns,
            transcendentals=0,
        ),
    )(hidden, gain, weight, adapter, chip)


def attend_kernel(
    length_ref, query_ref, cos_ref, sin_ref, new_ref, cache_ref, out_ref
):
    count = query_ref.shape[0]
    lanes = KV_HEADS * HEAD_WIDTH
    pad = new_ref.shape[1]
    first = pl.program_id(0) * count
    factor = HEAD_WIDTH ** (-0.5)
    row = lax.broadcasted_iota(jnp.int32, (2 * HEADS, lanes), 0)
    lane = lax.broadcasted_iota(jnp.int32, (2 * HEADS, lanes), 1)
    own = (row // GROUP) % KV_HEADS == lane // HEAD_WIDTH
    key_at = lax.broadcasted_iota(jnp.int32, (2 * HEADS, CACHE), 1)
    new_at = lax.broadcasted_iota(jnp.int32, (2 * HEADS, pad), 1)
    new_limit = lax.broadcasted_iota(jnp.int32, (2 * HEADS, pad), 0) // HEADS
    across = (((1,), (1,)), ((), ()))
    for b in range(count):
        query = query_ref[b].astype(jnp.float32)
        turned = pltpu.roll(query, HEAD_WIDTH // 2, 1)
        rotated = jnp.concatenate(
            [
                query[p * HEADS : (p + 1) * HEADS] * cos_ref[b, p : p + 1, :]
                + turned[p * HEADS : (p + 1) * HEADS] * sin_ref[b, p : p + 1, :]
                for p in range(2)
            ],
            axis=0,
        ).astype(jnp.bfloat16)
        wide = jnp.concatenate([rotated] * KV_HEADS, axis=1)
        wide = jnp.where(own, wide, jnp.zeros((), jnp.bfloat16))
        old = (
            lax.dot_general(
                wide, cache_ref[b, :, 0:lanes], across, preferred_element_type=jnp.float32
            )
            * factor
        )
        new = (
            lax.dot_general(
                wide, new_ref[b, :, 0:lanes], across, preferred_element_type=jnp.float32
            )
            * factor
        )
        old = jnp.where(key_at < length_ref[first + b], old, masked_out)
        new = jnp.where(new_at <= new_limit, new, masked_out)
        highest = jnp.maximum(
            jnp.max(old, axis=1, keepdims=True), jnp.max(new, axis=1, keepdims=True)
        )
        old_exp = jnp.exp(old - highest)
        new_exp = jnp.exp(new - highest)
        denominator = jnp.sum(old_exp, axis=1, keepdims=True) + jnp.sum(
            new_exp, axis=1, keepdims=True
        )
        old_weights = (old_exp / denominator).astype(jnp.bfloat16)
        new_weights = (new_exp / denominator).astype(jnp.bfloat16)
        mixture = jnp.dot(
            old_weights, cache_ref[b, :, lanes:], preferred_element_type=jnp.float32
        ) + jnp.dot(new_weights, new_ref[b, :, lanes:], preferred_element_type=jnp.float32)
        pieces = []
        for p in range(2):
            for g in range(KV_HEADS):
                start = p * HEADS + g * GROUP
                pieces.append(
                    mixture[start : start + GROUP, g * HEAD_WIDTH : (g + 1) * HEAD_WIDTH]
                )
        out_ref[b] = jnp.concatenate(pieces, axis=0).astype(jnp.bfloat16)


def attend_rows(lengths, query, cosine, sine, new, cache):
    requests = query.shape[0]
    block = 4

    def spec(*shape):
        return pl.BlockSpec((block,) + shape, lambda i: (i,) + (0,) * len(shape))

    return pl.pallas_call(
        attend_kernel,
        grid=(requests // block,),
        out_shape=jax.ShapeDtypeStruct((requests, 2 * HEADS, HEAD_WIDTH), jnp.bfloat16),
        in_specs=[
            pl.BlockSpec(memory_space=pltpu.SMEM),
            spec(2 * HEADS, HEAD_WIDTH),
            spec(2, HEAD_WIDTH),
            spec(2, HEAD_WIDTH),
            spec(new.shape[1], new.shape[2]),
            spec(CACHE, cache.shape[2]),
        ],
        out_specs=spec(2 * HEADS, HEAD_WIDTH),
        compiler_params=pltpu.CompilerParams(vmem_limit_bytes=32 * 1024 * 1024),
        cost_estimate=pl.CostEstimate(
            flops=4 * requests * 2 * HEADS * HEAD_WIDTH * CACHE * KV_HEADS,
            bytes_accessed=2 * requests * CACHE * cache.shape[2],
            transcendentals=requests * 2 * HEADS * CACHE,
        ),
    )(lengths, query, cosine, sine, new, cache)


def ring_body(
    tp_count,
    dp_count,
    hidden,
    norm_gain,
    w_qkv,
    adapter_store,
    adapter_home,
    slot_adapter,
    request_slot,
    cache_kv,
    cache_len,
):
    tp_index = lax.axis_index("tp")
    dp_index = lax.axis_index("dp")
    requests = hidden.shape[1]
    local_width = hidden.shape[3]
    device_heads = w_qkv.shape[1]
    local_requests = requests // tp_count
    rows = requests * 2
    column_start = tp_index * local_width

    per_chip = dp_count * ADAPT_DEV
    stored_rows = adapter_home[slot_adapter]
    slot_chip = stored_rows // per_chip
    within = jnp.sum(jnp.where(slot_chip == tp_index, stored_rows % per_chip, 0), axis=1)
    holder, local_slot = within // ADAPT_DEV, within % ADAPT_DEV
    other = 1 - dp_index
    mine = lax.dynamic_index_in_dim(adapter_store, local_slot[dp_index], 0, keepdims=False)
    theirs = lax.dynamic_index_in_dim(adapter_store, local_slot[other], 0, keepdims=False)
    swapped = lax.ppermute(theirs, "dp", [(0, 1), (1, 0)])
    adapter = jnp.where(holder[dp_index] == dp_index, mine, swapped)
    slots = jnp.arange(slot_adapter.shape[1], dtype=jnp.int32)
    block_chip = lax.dynamic_index_in_dim(slot_chip, dp_index, 0, keepdims=False)
    request_chip = jnp.sum(
        jnp.where(request_slot[0][:, None] == slots, block_chip, 0), axis=1, dtype=jnp.int32
    )
    row_chip = jnp.repeat(request_chip, 2)
    chip = jnp.broadcast_to(row_chip[:, None], (rows, 128))

    shared_width = device_heads * KEY_VALUE_SHARE
    weight = jnp.transpose(w_qkv, (1, 2, 0))
    gain = lax.dynamic_slice_in_dim(norm_gain, column_start, local_width, 0)
    gain = gain.astype(jnp.float32)[None, :]
    query, shared = project_rows(
        tp_count, hidden[0].reshape(rows, local_width), gain, weight, adapter.T, chip
    )
    query = query.reshape(tp_count, local_requests, 2, device_heads, HEAD_WIDTH)
    query = jnp.transpose(query, (1, 2, 0, 3, 4)).reshape(local_requests, 2 * HEADS, HEAD_WIDTH)
    shared = jnp.transpose(
        shared.reshape(tp_count, local_requests, 2, shared_width), (1, 2, 0, 3)
    ).reshape(local_requests, 2, HEADS * KEY_VALUE_SHARE)
    half = KV_HEADS * HEAD_WIDTH
    lengths = cache_len[0]
    positions = (lengths[:, None] + jnp.arange(2, dtype=jnp.int32)[None, :]).astype(jnp.float32)
    counter = jnp.arange(HEAD_WIDTH // 2, dtype=jnp.float32)
    inverse_freq = rope_base ** (-2.0 * counter / HEAD_WIDTH)
    angles = positions[..., None] * inverse_freq
    cosine, sine = jnp.cos(angles), jnp.sin(angles)
    cos_wide = jnp.concatenate([cosine, cosine], axis=-1)
    sin_wide = jnp.concatenate([-sine, sine], axis=-1)
    key_new = shared[..., :half].reshape(local_requests, 2, KV_HEADS, HEAD_WIDTH)
    key_wide = key_new.astype(jnp.float32)
    key_turned = jnp.roll(key_wide, HEAD_WIDTH // 2, axis=-1)
    key_rot = (
        key_wide * cos_wide[:, :, None, :] + key_turned * sin_wide[:, :, None, :]
    ).astype(jnp.bfloat16)
    new_kv = jnp.concatenate(
        [key_rot.reshape(local_requests, 2, half), shared[..., half:]], axis=-1
    )
    new_padded = jnp.pad(new_kv, ((0, 0), (0, 14), (0, 0)))
    attended = attend_rows(lengths, query, cos_wide, sin_wide, new_padded, cache_kv[0])
    attn_out = attended.reshape(local_requests, 2, HEADS * HEAD_WIDTH)
    return (attn_out[None], new_kv[None])


def body(tp_count, dp_count, hidden, norm_gain, w_qkv, *rest):
    rows = hidden.shape[1] * 2
    shared_width = w_qkv.shape[1] * KEY_VALUE_SHARE
    fits = (
        dp_count == 2
        and tp_count % 2 == 0
        and rows % (tp_count * 16) == 0
        and rows % 128 == 0
        and rows <= 1024
        and hidden.shape[3] % 128 == 0
        and shared_width % 128 == 0
        and (rows // 2) % (SPLIT * 16) == 0
    )
    if fits:
        return ring_body(tp_count, dp_count, hidden, norm_gain, w_qkv, *rest)
    return plain_body(hidden, norm_gain, w_qkv, *rest)


def solution(mesh):
    placed = (
        P(("group", "dp"), None, None, "tp"),
        P(),
        P(None, "tp", None),
        P(("group", "tp", "dp"), None, None),
        P("group"),
        P("group", None),
        P(("group", "dp"), None),
        P(("group", "dp"), "tp", None, None),
        P(("group", "dp"), "tp"),
    )
    return jax.shard_map(
        functools.partial(body, mesh.shape["tp"], mesh.shape["dp"]),
        mesh=mesh,
        in_specs=placed,
        out_specs=(P(("group", "dp"), "tp", None, None), P(("group", "dp"), "tp", None, None)),
        check_vma=False,
    )
```

```python
import functools

import jax
import jax.numpy as jnp
from jax import lax
from jax.experimental import pallas as pl
from jax.experimental.pallas import tpu as pltpu
from jax.sharding import PartitionSpec as P

D = 8192
HEADS = 64
KV_HEADS = 8
HEAD_WIDTH = 128
RANK = 64
CACHE = 128
ADAPT_DEV = 3
KEY_VALUE_SHARE = 32
GROUP = 8


adapter_scale = 0.0625
rope_base = 500000.0
norm_eps = 1e-05
masked_out = -1e30


def rotate(vectors, positions):
    halfway = vectors.shape[-1] // 2
    counter = jnp.arange(halfway, dtype=jnp.float32)
    inverse_freq = rope_base ** (-2.0 * counter / vectors.shape[-1])
    angles = positions[..., None] * inverse_freq
    cosine = jnp.cos(angles)
    sine_part = jnp.sin(angles)
    leading = vectors[..., :halfway]
    trailing = vectors[..., halfway:]
    return jnp.concatenate(
        [leading * cosine - trailing * sine_part, trailing * cosine + leading * sine_part], axis=-1
    )


def attend(query_rot, key_rot, value_new, cache_block, length_block):
    batch_count = query_rot.shape[0]
    grouped = query_rot.reshape(batch_count, 2, KV_HEADS, GROUP, HEAD_WIDTH)
    cache_keys = cache_block[:, :, : KV_HEADS * HEAD_WIDTH].reshape(
        batch_count, CACHE, KV_HEADS, HEAD_WIDTH
    )
    cache_values = cache_block[:, :, KV_HEADS * HEAD_WIDTH :].reshape(
        batch_count, CACHE, KV_HEADS, HEAD_WIDTH
    )
    factor = HEAD_WIDTH ** (-0.5)
    old_scores = (
        jnp.einsum("rpgjc,rlgc->rpgjl", grouped, cache_keys, preferred_element_type=jnp.float32)
        * factor
    )
    new_scores = (
        jnp.einsum("rpgjc,rngc->rpgjn", grouped, key_rot, preferred_element_type=jnp.float32)
        * factor
    )
    old_valid = jnp.arange(CACHE, dtype=jnp.int32)[None, :] < length_block[:, None]
    new_valid = jnp.arange(2, dtype=jnp.int32)[None, :] <= jnp.arange(2, dtype=jnp.int32)[:, None]
    old_scores = jnp.where(old_valid[:, None, None, None, :], old_scores, masked_out)
    new_scores = jnp.where(new_valid[None, :, None, None, :], new_scores, masked_out)
    highest = jnp.maximum(jnp.max(old_scores, axis=-1), jnp.max(new_scores, axis=-1))[..., None]
    old_exp = jnp.exp(old_scores - highest)
    new_exp = jnp.exp(new_scores - highest)
    denominator = jnp.sum(old_exp, axis=-1, keepdims=True) + jnp.sum(
        new_exp, axis=-1, keepdims=True
    )
    old_weights = (old_exp / denominator).astype(jnp.bfloat16)
    new_weights = (new_exp / denominator).astype(jnp.bfloat16)
    mixture = jnp.einsum(
        "rpgjl,rlgc->rpgjc", old_weights, cache_values, preferred_element_type=jnp.float32
    )
    mixture = mixture + jnp.einsum(
        "rpgjn,rngc->rpgjc", new_weights, value_new, preferred_element_type=jnp.float32
    )
    return mixture.astype(jnp.bfloat16).reshape(batch_count, 2, HEADS * HEAD_WIDTH)


def slot_delta(slot_slices, local_normed, chosen, count_of_rows, slot_count, local_width):
    down_matrix = jnp.transpose(slot_slices[:, :, :RANK], (1, 0, 2)).reshape(
        local_width, slot_count * RANK
    )
    partial_rank = jnp.dot(local_normed, down_matrix, preferred_element_type=jnp.float32).reshape(
        count_of_rows, slot_count, RANK
    )
    partial_rank = jnp.sum(jnp.where(chosen[:, :, None], partial_rank, 0.0), axis=1)
    lowrank = lax.psum(partial_rank, "tp").astype(jnp.bfloat16)
    spread = jnp.where(
        chosen[:, :, None], lowrank[:, None, :], jnp.zeros((), jnp.bfloat16)
    ).reshape(count_of_rows, slot_count * RANK)
    up_matrix = jnp.transpose(slot_slices[:, :, RANK:], (0, 2, 1)).reshape(
        slot_count * RANK, local_width
    )
    return jnp.dot(spread, up_matrix, preferred_element_type=jnp.float32)


def plain_body(
    hidden,
    norm_gain,
    w_qkv,
    adapter_store,
    adapter_home,
    slot_adapter,
    request_slot,
    cache_kv,
    cache_len,
):
    tp_count = lax.axis_size("tp")
    dp_count = lax.axis_size("dp")
    tp_index = lax.axis_index("tp")
    dp_index = lax.axis_index("dp")
    requests = hidden.shape[1]
    local_width = hidden.shape[3]
    device_heads = w_qkv.shape[1]
    slot_count = slot_adapter.shape[1]
    count_of_rows = requests * 2
    flat_rows = hidden[0].reshape(count_of_rows, local_width)
    gain_wide = norm_gain.astype(jnp.float32)
    weights = w_qkv.reshape(D, device_heads * (HEAD_WIDTH + KEY_VALUE_SHARE))
    column_start = tp_index * local_width
    stored_rows = adapter_home[slot_adapter]
    block_rows = lax.dynamic_index_in_dim(stored_rows, dp_index, 0, keepdims=False)
    device_index = tp_index * dp_count + dp_index
    offsets = stored_rows - device_index * ADAPT_DEV
    local_slots = jnp.arange(ADAPT_DEV, dtype=jnp.int32)
    selector = jnp.any(offsets[:, :, None] == local_slots[None, None, :], axis=1).astype(
        jnp.bfloat16
    )
    row_slot = jnp.repeat(request_slot[0], 2)
    chosen = row_slot[:, None] == jnp.arange(slot_count, dtype=jnp.int32)[None, :]
    gathered = lax.all_gather(flat_rows, "tp", axis=1, tiled=True)
    widened = gathered.astype(jnp.float32)
    mean_square = jnp.mean(widened * widened, axis=1, keepdims=True)
    normed = (widened * lax.rsqrt(mean_square + norm_eps) * gain_wide).astype(jnp.bfloat16)
    local_normed = lax.dynamic_slice_in_dim(normed, column_start, local_width, 1)
    projected_whole = jnp.dot(normed, weights, preferred_element_type=jnp.float32)
    pieces = adapter_store.reshape(ADAPT_DEV, tp_count, local_width, 2 * RANK)
    outgoing = jnp.einsum(
        "bm,mtlk->tblk", selector, pieces, preferred_element_type=jnp.float32
    ).astype(jnp.bfloat16)
    outgoing = outgoing.reshape(tp_count * dp_count, local_width, 2 * RANK)
    incoming = lax.all_to_all(outgoing, ("tp", "dp"), split_axis=0, concat_axis=0, tiled=True)
    slot_slices = jnp.take(incoming, block_rows // ADAPT_DEV, axis=0)
    delta_query = slot_delta(
        slot_slices, local_normed, chosen, count_of_rows, slot_count, local_width
    )
    delta_padded_rows = jnp.pad(
        delta_query.reshape(count_of_rows, device_heads, HEAD_WIDTH),
        ((0, 0), (0, 0), (0, KEY_VALUE_SHARE)),
    )
    packed_columns = (
        projected_whole.reshape(count_of_rows, device_heads, HEAD_WIDTH + KEY_VALUE_SHARE)
        + adapter_scale * delta_padded_rows
    ).astype(jnp.bfloat16)
    packed_columns = packed_columns.reshape(requests, 2, device_heads, HEAD_WIDTH + KEY_VALUE_SHARE)
    arrived_heads = lax.all_to_all(packed_columns, "tp", split_axis=0, concat_axis=2, tiled=True)
    local_requests = arrived_heads.shape[0]
    query_part = arrived_heads[..., :HEAD_WIDTH]
    shared = arrived_heads[..., HEAD_WIDTH:].reshape(local_requests, 2, HEADS * KEY_VALUE_SHARE)
    key_new = shared[..., : KV_HEADS * HEAD_WIDTH].reshape(local_requests, 2, KV_HEADS, HEAD_WIDTH)
    value_new = shared[..., KV_HEADS * HEAD_WIDTH :].reshape(
        local_requests, 2, KV_HEADS, HEAD_WIDTH
    )
    lengths = cache_len[0]
    positions = (lengths[:, None] + jnp.arange(2, dtype=jnp.int32)[None, :]).astype(jnp.float32)
    query_rot = rotate(query_part.astype(jnp.float32), positions[..., None]).astype(jnp.bfloat16)
    key_rot = rotate(key_new.astype(jnp.float32), positions[..., None]).astype(jnp.bfloat16)
    attn_out = attend(query_rot, key_rot, value_new, cache_kv[0], lengths)
    new_kv = jnp.concatenate(
        [
            key_rot.reshape(local_requests, 2, KV_HEADS * HEAD_WIDTH),
            value_new.reshape(local_requests, 2, KV_HEADS * HEAD_WIDTH),
        ],
        axis=-1,
    )
    return (attn_out[None], new_kv[None])


SPLIT = 2
COLUMN_TILE = 256
MESH_ID = pl.DeviceIdType.MESH


def ring_to_tp(place, n):
    high = place // (n // 2)
    return (1 - high) * (2 * place) + high * (2 * (n - 1 - place) + 1)


def project_kernel(
    n,
    hidden_ref,
    gain_ref,
    weight_ref,
    adapter_ref,
    chip_ref,
    query_out,
    shared_out,
    normed,
    weight_buf,
    total,
    query_send,
    shared_send,
    up_all,
    sums_send,
    sums_all,
    reduce_send,
    reduce_recv,
    lowrank_all,
    weight_sem,
    ring_send,
    ring_recv,
    sums_send_sem,
    sums_recv_sem,
    up_send_sem,
    up_recv_sem,
    reduce_send_sem,
    reduce_recv_sem,
    spread_send_sem,
    spread_recv_sem,
    shared_send_sem,
    shared_recv_sem,
    query_send_sem,
    query_recv_sem,
):
    me = lax.axis_index("tp")
    rows, width = hidden_ref.shape
    own_rows = rows // n
    query_width = query_send.shape[1]
    shared_width = shared_send.shape[1]
    piece = rows // 2 // SPLIT

    def peer(d):
        return lax.rem(me + d, n)

    def source(d):
        return lax.rem(me + n - d, n)

    def rows_of(t):
        return pl.ds(pl.multiple_of(t * own_rows, own_rows), own_rows)

    def remote(src, dst, send_sem, recv_sem, target):
        return pltpu.make_async_remote_copy(
            src_ref=src,
            dst_ref=dst,
            send_sem=send_sem,
            recv_sem=recv_sem,
            device_id={"tp": target},
            device_id_type=MESH_ID,
        )

    barrier = pltpu.get_barrier_semaphore()
    for d in range(1, n):
        pl.semaphore_signal(barrier, inc=1, device_id={"tp": peer(d)}, device_id_type=MESH_ID)

    heads = weight_ref.shape[0]
    low_column = query_width + shared_width
    adapter_copy = pltpu.make_async_copy(
        adapter_ref, weight_buf.at[pl.ds(low_column, 2 * RANK)], weight_sem.at[2 * heads]
    )
    adapter_copy.start()

    def weight_copies(head):
        return (
            pltpu.make_async_copy(
                weight_ref.at[head, pl.ds(0, HEAD_WIDTH)],
                weight_buf.at[pl.ds(head * HEAD_WIDTH, HEAD_WIDTH)],
                weight_sem.at[2 * head],
            ),
            pltpu.make_async_copy(
                weight_ref.at[head, pl.ds(HEAD_WIDTH, KEY_VALUE_SHARE)],
                weight_buf.at[pl.ds(query_width + head * KEY_VALUE_SHARE, KEY_VALUE_SHARE)],
                weight_sem.at[2 * head + 1],
            ),
        )

    for head in range(heads):
        for copy in weight_copies(head):
            copy.start()

    sums_send[...] = jnp.zeros_like(sums_send)
    for i in range(rows // 128):
        wide = hidden_ref[i * 128 : (i + 1) * 128, :].astype(jnp.float32)
        square = jnp.sum(wide * wide, axis=1, keepdims=True)
        sums_send[i : i + 1, :] = jnp.transpose(jnp.broadcast_to(square, (128, 128)))[0:1, :]
    sums_all[me] = sums_send[...]
    pl.semaphore_wait(barrier, n - 1)

    def sums_copy(d):
        return remote(
            sums_send, sums_all.at[me], sums_send_sem.at[d], sums_recv_sem.at[d], peer(d)
        )

    def up_slice(t):
        features = pl.ds(pl.multiple_of(t * width, width), width)
        return weight_buf.at[pl.ds(low_column + RANK, RANK), features]

    def up_copy(d):
        return remote(
            up_slice(peer(d)), up_all.at[me], up_send_sem.at[d], up_recv_sem.at[d], peer(d)
        )

    for d in range(1, n):
        sums_copy(d).start()
    adapter_copy.wait()
    for d in range(1, n):
        up_copy(d).start()
    up_all[me] = up_slice(me)[...]
    for d in range(1, n):
        sums_copy(d).wait_recv()
    sums = sums_all[0]
    for t in range(1, n):
        sums = sums + sums_all[t]
    scale = lax.rsqrt(sums / (n * width) + norm_eps)
    for i in range(rows // 128):
        span = slice(i * 128, (i + 1) * 128)
        column = jnp.transpose(jnp.broadcast_to(scale[i : i + 1, :], (128, 128)))[:, 0:1]
        wide = hidden_ref[span, :].astype(jnp.float32)
        normed[me, span, :] = (wide * column * gain_ref[...]).astype(jnp.bfloat16)

    odd = lax.rem(me, 2)
    place = (1 - odd) * (me // 2) + odd * ((2 * n - 1 - me) // 2)
    right = ring_to_tp(lax.rem(place + 1, n), n)
    left = ring_to_tp(lax.rem(place + n - 1, n), n)

    def ring_part(direction, i):
        step, part = i // SPLIT, i % SPLIT
        if direction == 0:
            owner = ring_to_tp(lax.rem(place + n - step, n), n)
        else:
            owner = ring_to_tp(lax.rem(place + step, n), n)
        start = direction * (rows // 2) + part * piece
        if not isinstance(start, int):
            start = pl.multiple_of(start, piece)
        return owner, pl.ds(start, piece)

    def ring_copy(direction, i):
        owner, span = ring_part(direction, i)
        block = normed.at[owner, span]
        return remote(
            block,
            block,
            ring_send.at[direction, i],
            ring_recv.at[direction, i],
            left if direction else right,
        )

    def compute(i):
        parts = [ring_part(direction, i) for direction in range(2)]

        def add(columns):
            for owner, span in parts:
                features = pl.ds(pl.multiple_of(owner * width, width), width)
                total[span, columns] += lax.dot_general(
                    normed[owner, span, :],
                    weight_buf[columns, features],
                    (((1,), (1,)), ((), ())),
                    preferred_element_type=jnp.float32,
                )

        @pl.loop(0, low_column // COLUMN_TILE)
        def _(j):
            add(pl.ds(pl.multiple_of(j * COLUMN_TILE, COLUMN_TILE), COLUMN_TILE))

        add(pl.ds(low_column, 2 * RANK))

    for i in range(SPLIT):
        for direction in range(2):
            ring_copy(direction, i).start()

    total[...] = jnp.zeros_like(total)
    for head in range(heads):
        for copy in weight_copies(head):
            copy.wait()

    def first(i, _):
        compute(i)
        return 0

    lax.fori_loop(0, SPLIT, first, 0)

    def middle(i, _):
        for direction in range(2):
            ring_copy(direction, i - SPLIT).wait_recv()
            ring_copy(direction, i).start()
        compute(i)
        return 0

    lax.fori_loop(SPLIT, (n - 1) * SPLIT, middle, 0)

    def last(i, _):
        for direction in range(2):
            ring_copy(direction, i - SPLIT).wait_recv()
        compute(i)
        return 0

    lax.fori_loop((n - 1) * SPLIT, n * SPLIT, last, 0)

    lane = lax.broadcasted_iota(jnp.int32, (own_rows, 128), 1)
    for t in range(n):
        span = slice(t * own_rows, (t + 1) * own_rows)
        low = total[span, low_column : low_column + 128]
        reduce_send[span, :] = jnp.where(
            (chip_ref[span, :] == me) & (lane < RANK), low, 0.0
        ).astype(jnp.bfloat16)

    def reduce_copy(d):
        return remote(
            reduce_send.at[rows_of(peer(d))],
            reduce_recv.at[me],
            reduce_send_sem.at[d],
            reduce_recv_sem.at[d],
            peer(d),
        )

    for d in range(1, n):
        reduce_copy(d).start()
    reduce_recv[me] = reduce_send[rows_of(me), :]

    shared_send[...] = total[:, query_width:low_column].astype(jnp.bfloat16)

    def shared_copy(d):
        return remote(
            shared_send.at[rows_of(peer(d))],
            shared_out.at[me],
            shared_send_sem.at[d],
            shared_recv_sem.at[d],
            peer(d),
        )

    for d in range(1, n):
        reduce_copy(d).wait_recv()
    low = reduce_recv[0].astype(jnp.float32)
    for t in range(1, n):
        low = low + reduce_recv[t].astype(jnp.float32)
    lowrank_all[me] = low.astype(jnp.bfloat16)

    def spread_copy(d):
        return remote(
            lowrank_all.at[me],
            lowrank_all.at[me],
            spread_send_sem.at[d],
            spread_recv_sem.at[d],
            peer(d),
        )

    for d in range(1, n):
        spread_copy(d).start()
    for d in range(1, n):
        shared_copy(d).start()
    shared_out[me] = shared_send[rows_of(me), :]
    for d in range(1, n):
        up_copy(d).wait_recv()
    for d in range(1, n):
        spread_copy(d).wait_recv()

    def mixed(t):
        low = lowrank_all[t].astype(jnp.float32)
        chip = chip_ref[rows_of(t), :]
        tiles = []
        for pair in range(n // 2):
            even_part = jnp.where(chip == 2 * pair, low, 0.0)
            odd_part = jnp.where(chip == 2 * pair + 1, low, 0.0)
            tiles.append((even_part + pltpu.roll(odd_part, RANK, 1)).astype(jnp.bfloat16))
        spread = jnp.concatenate(tiles, axis=1)
        up = up_all[...].reshape(n * RANK, query_width)
        delta = jnp.dot(spread, up, preferred_element_type=jnp.float32)
        query = total[rows_of(t), 0:query_width]
        return (query + adapter_scale * delta).astype(jnp.bfloat16)

    def query_copy(d):
        return remote(
            query_send.at[rows_of(peer(d))],
            query_out.at[me],
            query_send_sem.at[d],
            query_recv_sem.at[d],
            peer(d),
        )

    def send_query(d, _):
        query_send[rows_of(peer(d)), :] = mixed(peer(d))
        query_copy(d).start()
        return 0

    lax.fori_loop(1, n, send_query, 0)
    query_out[me] = mixed(me)

    for d in range(1, n):
        shared_copy(d).wait_recv()
        query_copy(d).wait_recv()

    def drain(i, _):
        for direction in range(2):
            ring_copy(direction, i).wait_send()
        return 0

    lax.fori_loop(0, (n - 1) * SPLIT, drain, 0)
    for d in range(1, n):
        sums_copy(d).wait_send()
        up_copy(d).wait_send()
        reduce_copy(d).wait_send()
        spread_copy(d).wait_send()
        shared_copy(d).wait_send()
        query_copy(d).wait_send()


def project_rows(n, hidden, gain, weight, adapter, chip):
    rows, width = hidden.shape
    heads = weight.shape[0]
    own_rows = rows // n
    query_width = heads * HEAD_WIDTH
    shared_width = heads * KEY_VALUE_SHARE
    columns = query_width + shared_width + 2 * RANK
    dma = pltpu.SemaphoreType.DMA
    vmem = pl.BlockSpec(memory_space=pltpu.VMEM)
    hbm = pl.BlockSpec(memory_space=pl.ANY)
    bf16, f32 = jnp.bfloat16, jnp.float32
    return pl.pallas_call(
        functools.partial(project_kernel, n),
        out_shape=(
            jax.ShapeDtypeStruct((n, own_rows, query_width), bf16),
            jax.ShapeDtypeStruct((n, own_rows, shared_width), bf16),
        ),
        in_specs=[vmem, vmem, hbm, hbm, vmem],
        out_specs=(vmem, vmem),
        scratch_shapes=[
            pltpu.VMEM((n, rows, width), bf16),
            pltpu.VMEM((columns, n * width), bf16),
            pltpu.VMEM((rows, columns), f32),
            pltpu.VMEM((rows, query_width), bf16),
            pltpu.VMEM((rows, shared_width), bf16),
            pltpu.VMEM((n, RANK, query_width), bf16),
            pltpu.VMEM((8, 128), f32),
            pltpu.VMEM((n, 8, 128), f32),
            pltpu.VMEM((rows, 128), bf16),
            pltpu.VMEM((n, own_rows, 128), bf16),
            pltpu.VMEM((n, own_rows, 128), bf16),
            dma((2 * heads + 1,)),
            dma((2, (n - 1) * SPLIT)),
            dma((2, (n - 1) * SPLIT)),
        ]
        + [dma((n,))] * 12,
        compiler_params=pltpu.CompilerParams(
            collective_id=0, has_side_effects=True, vmem_limit_bytes=60 * 1024 * 1024
        ),
        cost_estimate=pl.CostEstimate(
            flops=2 * rows * width * n * columns,
            bytes_accessed=2 * n * width * columns,
            transcendentals=0,
        ),
    )(hidden, gain, weight, adapter, chip)


CACHE_PARTS = 4


def attend_kernel(length_ref, query_ref, cos_ref, sin_ref, new_ref, *rest):
    cache_refs, out_ref = rest[:CACHE_PARTS], rest[CACHE_PARTS]
    count = query_ref.shape[0]
    lanes = KV_HEADS * HEAD_WIDTH
    part_width = 2 * lanes // CACHE_PARTS
    pad = new_ref.shape[1]
    first = pl.program_id(0) * count
    factor = HEAD_WIDTH ** (-0.5)
    group_rows = 2 * GROUP
    key_at = lax.broadcasted_iota(jnp.int32, (2 * HEADS, CACHE), 1)
    new_at = lax.broadcasted_iota(jnp.int32, (2 * HEADS, pad), 1)
    new_limit = (lax.broadcasted_iota(jnp.int32, (2 * HEADS, pad), 0) // GROUP) % 2
    second = (lax.broadcasted_iota(jnp.int32, (2 * HEADS, HEAD_WIDTH), 0) // GROUP) % 2 == 1
    across = (((1,), (1,)), ((), ()))

    def cached(b, start):
        within = start % part_width
        return cache_refs[start // part_width][b, :, within : within + HEAD_WIDTH]

    for b in range(count):
        query = query_ref[b].astype(jnp.float32)
        turned = pltpu.roll(query, HEAD_WIDTH // 2, 1)
        cosine = jnp.where(second, cos_ref[b, 1:2, :], cos_ref[b, 0:1, :])
        sine = jnp.where(second, sin_ref[b, 1:2, :], sin_ref[b, 0:1, :])
        rotated = (query * cosine + turned * sine).astype(jnp.bfloat16)
        old, new = [], []
        for g in range(KV_HEADS):
            own = rotated[g * group_rows : (g + 1) * group_rows]
            start = g * HEAD_WIDTH
            old.append(
                lax.dot_general(
                    own, cached(b, start), across, preferred_element_type=jnp.float32
                )
            )
            new.append(
                lax.dot_general(
                    own,
                    new_ref[b, :, start : start + HEAD_WIDTH],
                    across,
                    preferred_element_type=jnp.float32,
                )
            )
        old = jnp.concatenate(old, axis=0) * factor
        new = jnp.concatenate(new, axis=0) * factor
        old = jnp.where(key_at < length_ref[first + b], old, masked_out)
        new = jnp.where(new_at <= new_limit, new, masked_out)
        highest = jnp.maximum(
            jnp.max(old, axis=1, keepdims=True), jnp.max(new, axis=1, keepdims=True)
        )
        old_exp = jnp.exp(old - highest)
        new_exp = jnp.exp(new - highest)
        denominator = jnp.sum(old_exp, axis=1, keepdims=True) + jnp.sum(
            new_exp, axis=1, keepdims=True
        )
        old_weights = (old_exp / denominator).astype(jnp.bfloat16)
        new_weights = (new_exp / denominator).astype(jnp.bfloat16)
        for g in range(KV_HEADS):
            span = slice(g * group_rows, (g + 1) * group_rows)
            start = lanes + g * HEAD_WIDTH
            mixture = jnp.dot(
                old_weights[span], cached(b, start), preferred_element_type=jnp.float32
            ) + jnp.dot(
                new_weights[span],
                new_ref[b, :, start : start + HEAD_WIDTH],
                preferred_element_type=jnp.float32,
            )
            out_ref[b, span, :] = mixture.astype(jnp.bfloat16)


def attend_rows(lengths, query, cosine, sine, new, cache):
    requests = query.shape[0]
    block = 8
    width = cache.shape[2] // CACHE_PARTS

    def spec(*shape):
        return pl.BlockSpec((block,) + shape, lambda i: (i,) + (0,) * len(shape))

    def cache_spec(part):
        return pl.BlockSpec((block, CACHE, width), lambda i: (i, 0, part))

    return pl.pallas_call(
        attend_kernel,
        grid=(requests // block,),
        out_shape=jax.ShapeDtypeStruct((requests, 2 * HEADS, HEAD_WIDTH), jnp.bfloat16),
        in_specs=[
            pl.BlockSpec(memory_space=pltpu.SMEM),
            spec(2 * HEADS, HEAD_WIDTH),
            spec(2, HEAD_WIDTH),
            spec(2, HEAD_WIDTH),
            spec(new.shape[1], new.shape[2]),
        ]
        + [cache_spec(part) for part in range(CACHE_PARTS)],
        out_specs=spec(2 * HEADS, HEAD_WIDTH),
        compiler_params=pltpu.CompilerParams(vmem_limit_bytes=48 * 1024 * 1024),
        cost_estimate=pl.CostEstimate(
            flops=4 * requests * 2 * HEADS * HEAD_WIDTH * CACHE,
            bytes_accessed=2 * requests * CACHE * cache.shape[2],
            transcendentals=requests * 2 * HEADS * CACHE,
        ),
    )(lengths, query, cosine, sine, new, *([cache] * CACHE_PARTS))


def ring_body(
    tp_count,
    dp_count,
    hidden,
    norm_gain,
    w_qkv,
    adapter_store,
    adapter_home,
    slot_adapter,
    request_slot,
    cache_kv,
    cache_len,
):
    tp_index = lax.axis_index("tp")
    dp_index = lax.axis_index("dp")
    requests = hidden.shape[1]
    local_width = hidden.shape[3]
    device_heads = w_qkv.shape[1]
    local_requests = requests // tp_count
    rows = requests * 2
    column_start = tp_index * local_width

    per_chip = dp_count * ADAPT_DEV
    stored_rows = adapter_home[slot_adapter]
    slot_chip = stored_rows // per_chip
    within = jnp.sum(jnp.where(slot_chip == tp_index, stored_rows % per_chip, 0), axis=1)
    holder, local_slot = within // ADAPT_DEV, within % ADAPT_DEV
    other = 1 - dp_index
    mine = lax.dynamic_index_in_dim(adapter_store, local_slot[dp_index], 0, keepdims=False)
    theirs = lax.dynamic_index_in_dim(adapter_store, local_slot[other], 0, keepdims=False)
    swapped = lax.ppermute(theirs, "dp", [(0, 1), (1, 0)])
    adapter = jnp.where(holder[dp_index] == dp_index, mine, swapped)
    slots = jnp.arange(slot_adapter.shape[1], dtype=jnp.int32)
    block_chip = lax.dynamic_index_in_dim(slot_chip, dp_index, 0, keepdims=False)
    request_chip = jnp.sum(
        jnp.where(request_slot[0][:, None] == slots, block_chip, 0), axis=1, dtype=jnp.int32
    )
    row_chip = jnp.repeat(request_chip, 2)
    chip = jnp.broadcast_to(row_chip[:, None], (rows, 128))

    shared_width = device_heads * KEY_VALUE_SHARE
    weight = jnp.transpose(w_qkv, (1, 2, 0))
    gain = lax.dynamic_slice_in_dim(norm_gain, column_start, local_width, 0)
    gain = gain.astype(jnp.float32)[None, :]
    query, shared = project_rows(
        tp_count, hidden[0].reshape(rows, local_width), gain, weight, adapter.T, chip
    )
    query = query.reshape(
        tp_count, local_requests, 2, device_heads // GROUP, GROUP, HEAD_WIDTH
    )
    query = jnp.transpose(query, (1, 0, 3, 2, 4, 5)).reshape(
        local_requests, 2 * HEADS, HEAD_WIDTH
    )
    shared = jnp.transpose(
        shared.reshape(tp_count, local_requests, 2, shared_width), (1, 2, 0, 3)
    ).reshape(local_requests, 2, HEADS * KEY_VALUE_SHARE)
    half = KV_HEADS * HEAD_WIDTH
    lengths = cache_len[0]
    positions = (lengths[:, None] + jnp.arange(2, dtype=jnp.int32)[None, :]).astype(jnp.float32)
    counter = jnp.arange(HEAD_WIDTH // 2, dtype=jnp.float32)
    inverse_freq = rope_base ** (-2.0 * counter / HEAD_WIDTH)
    angles = positions[..., None] * inverse_freq
    cosine, sine = jnp.cos(angles), jnp.sin(angles)
    cos_wide = jnp.concatenate([cosine, cosine], axis=-1)
    sin_wide = jnp.concatenate([-sine, sine], axis=-1)
    key_new = shared[..., :half].reshape(local_requests, 2, KV_HEADS, HEAD_WIDTH)
    key_wide = key_new.astype(jnp.float32)
    key_turned = jnp.roll(key_wide, HEAD_WIDTH // 2, axis=-1)
    key_rot = (
        key_wide * cos_wide[:, :, None, :] + key_turned * sin_wide[:, :, None, :]
    ).astype(jnp.bfloat16)
    new_kv = jnp.concatenate(
        [key_rot.reshape(local_requests, 2, half), shared[..., half:]], axis=-1
    )
    new_padded = jnp.pad(new_kv, ((0, 0), (0, 14), (0, 0)))
    attended = attend_rows(lengths, query, cos_wide, sin_wide, new_padded, cache_kv[0])
    attended = attended.reshape(local_requests, KV_HEADS, 2, GROUP, HEAD_WIDTH)
    attn_out = jnp.transpose(attended, (0, 2, 1, 3, 4)).reshape(
        local_requests, 2, HEADS * HEAD_WIDTH
    )
    return (attn_out[None], new_kv[None])


def body(tp_count, dp_count, hidden, norm_gain, w_qkv, *rest):
    rows = hidden.shape[1] * 2
    shared_width = w_qkv.shape[1] * KEY_VALUE_SHARE
    fits = (
        dp_count == 2
        and tp_count % 2 == 0
        and rows % (tp_count * 16) == 0
        and rows % 128 == 0
        and rows <= 1024
        and hidden.shape[3] % 128 == 0
        and shared_width % 128 == 0
        and (rows // 2) % (SPLIT * 16) == 0
        and w_qkv.shape[1] % GROUP == 0
        and rows // (2 * tp_count) % 8 == 0
    )
    if fits:
        return ring_body(tp_count, dp_count, hidden, norm_gain, w_qkv, *rest)
    return plain_body(hidden, norm_gain, w_qkv, *rest)


def solution(mesh):
    placed = (
        P(("group", "dp"), None, None, "tp"),
        P(),
        P(None, "tp", None),
        P(("group", "tp", "dp"), None, None),
        P("group"),
        P("group", None),
        P(("group", "dp"), None),
        P(("group", "dp"), "tp", None, None),
        P(("group", "dp"), "tp"),
    )
    return jax.shard_map(
        functools.partial(body, mesh.shape["tp"], mesh.shape["dp"]),
        mesh=mesh,
        in_specs=placed,
        out_specs=(P(("group", "dp"), "tp", None, None), P(("group", "dp"), "tp", None, None)),
        check_vma=False,
    )
```
